512 devices in a mesh: row: 32 (over y_hi, z), col: 16 (over x, y_lo, core).
Axes of the slice: x: 4, y: 8 (y_hi: 4, y_lo: 2; y = y_hi * 2 + y_lo), z: 8, core: 2. Of those that a mesh axis runs over, the one named last changes fastest.
Arguments:
- positions: float32 [3, 262144], P(None, ('row', 'col')), as said below
- velocities: float32 [3, 262144], P(None, ('row', 'col')), may hold values from -2.5 to 2.5
- bead_types: int32 [262144], P(('row', 'col')), may hold values from 0 to 17
- slot_bead: int32 [262144], P(('row', 'col')), may hold values from 0 to 511, as said below
- tile_pairs: int32 [2, 36864], P(None, ('row', 'col')), may hold values from 0 to 127, as said below
- tile_count: int32 [512], P(('row', 'col')), may hold values from 1 to 72, as said below
- c6_table: float32 [18, 18], replicated, as said below
- c12_table: float32 [18, 18], replicated, as said below
Outputs:
- kicked: float32 [3, 262144], P(None, ('row', 'col'))
The draws below stay inside these ranges and needn't reach their ends.
Inputs may be any that keep to these rules, and one draw needn't show every extreme that they name: `positions`: the beads of block k of device d = r * 16 + c lie in the cell [u, u + 1) x [v, v + 1) x [k, k + 1), in units of 2.47 nm, with u = 2 (c % 8) + c // 8 and v = 2 (r % 16) + r // 16: a slab periodic in its first two dimensions. `slot_bead`: each device's values are a permutation of 0 to 511. `tile_pairs`: the first row is below 64, the second below 128; the 72 (i-block, j-block) pairs of a device are distinct, and the cells of the two blocks are equal or touch, counting periodic images in the first two dimensions. `tile_count`: A device's live tiles are its first slots. Of the two devices of a row whose col indices differ only in the lowest bit, one has 72 live tiles and the other at most 24; some pair reaches 24 in every draw. `c6_table`: Symmetric. `c12_table`: Symmetric.
All inputs are finite; a program needn't handle non-finite values.
Results may differ from the reference program's by a relative error of at most 0.0003.
Values sent between devices are 32-bit elements; how exact they have to be, the bound alone decides.
A program may use at most 64 MiB of HBM per device.

```python
import math
import jax
import jax.numpy as jnp
from jax import lax

BLOCK = 128
BPD = 4
P_DEV = 72
NTYPE = 18
NBEADS = 262144
P_LIGHT = 24
TILES = 36864
N_ROW = 32
N_COL = 16


CELL_SIDE = 2.47


def spread_cell(index, count):
    half = count // 2
    return 2 * (index % half) + index // half


def owner_cell(place, count):
    half = count // 2
    return place // 2 + place % 2 * half


def shared_slots(key):
    key = jax.random.fold_in(key, 77)
    keys = jax.random.split(key, N_ROW * N_COL)
    return jax.vmap(lambda k: jax.random.permutation(k, BPD * BLOCK))(keys).astype(jnp.int32)


def draw_positions(key, part):
    perms = shared_slots(key)
    key = jax.random.fold_in(key, 11)
    inverse = jnp.argsort(perms, axis=1).astype(jnp.int32)
    block = inverse // BLOCK
    device = jnp.arange(N_ROW * N_COL, dtype=jnp.int32)[:, None]
    cell_x = spread_cell(device % N_COL, N_COL) + 0 * block
    cell_y = spread_cell(device // N_COL, N_ROW) + 0 * block
    cells = jnp.stack([cell_x, cell_y, block]).reshape(3, -1).astype(jnp.float32)
    jitter = jax.random.uniform(key, cells.shape, jnp.float32, 0.0, 1.0)
    return ((cells + jitter) * CELL_SIDE).astype(jnp.float32)


def draw_slot_bead(key, part):
    perms = shared_slots(key)
    key = jax.random.fold_in(key, 12)
    return perms.reshape(-1).astype(jnp.int32)


def draw_tile_pairs(key, part):
    key = jax.random.fold_in(key, 13)
    keys = jax.random.split(key, N_ROW * N_COL)
    combos = 27 * BPD
    index = jnp.arange(combos, dtype=jnp.int32)
    shift_a = index % 3 - 1
    shift_b = index // 3 % 3 - 1
    shift_z = index // 9 % 3 - 1
    layer_a = index // 27
    layer_b = layer_a + shift_z
    valid = (layer_b >= 0) & (layer_b < BPD)

    def pick(k, device):
        row_at = device // N_COL
        col_at = device % N_COL
        score = jax.random.permutation(k, combos).astype(jnp.int32) + jnp.where(valid, 0, combos)
        chosen = jnp.argsort(score)[:P_DEV]
        place_x = (spread_cell(col_at, N_COL) + jnp.take(shift_a, chosen)) % N_COL
        place_y = (spread_cell(row_at, N_ROW) + jnp.take(shift_b, chosen)) % N_ROW
        col_a = owner_cell(place_x, N_COL)
        row_b = owner_cell(place_y, N_ROW)
        first = col_a * BPD + jnp.take(layer_a, chosen)
        second = row_b * BPD + jnp.take(layer_b, chosen)
        return (first, second)
    first, second = jax.vmap(pick)(keys, jnp.arange(N_ROW * N_COL, dtype=jnp.int32))
    return jnp.stack([first.reshape(-1), second.reshape(-1)]).astype(jnp.int32)


def draw_tile_count(key, part):
    key = jax.random.fold_in(key, 14)
    count_pairs = N_ROW * N_COL // 2
    key_light, key_forced, key_heavy = jax.random.split(key, 3)
    light = jax.random.randint(key_light, (count_pairs,), 1, P_LIGHT + 1)
    forced = jax.random.randint(key_forced, (), 0, count_pairs)
    light = jnp.where(jnp.arange(count_pairs) == forced, P_LIGHT, light)
    heavy = jax.random.randint(key_heavy, (count_pairs,), 0, 2)
    device = jnp.arange(N_ROW * N_COL)
    return jnp.where(device % 2 == heavy[device // 2], P_DEV, light[device // 2]).astype(jnp.int32)


def draw_c6_table(key, part):
    key = jax.random.fold_in(key, 15)
    values = jnp.exp(jax.random.uniform(key, (NTYPE, NTYPE), jnp.float32, math.log(0.05), math.log(0.3)))
    return ((values + values.T) * 0.5).astype(jnp.float32)


def draw_c12_table(key, part):
    key = jax.random.fold_in(key, 16)
    values = jnp.exp(jax.random.uniform(key, (NTYPE, NTYPE), jnp.float32, math.log(0.0005), math.log(0.003)))
    return ((values + values.T) * 0.5).astype(jnp.float32)


def place_ends(values, stream_key, least, top_value):
    spot = [jax.random.randint(jax.random.fold_in(stream_key, axis), (), 0, length) for axis, length in enumerate(values.shape)]
    main_axis = values.shape.index(max(values.shape))
    beside = spot[:main_axis] + [(spot[main_axis] + 1) % values.shape[main_axis]] + spot[main_axis + 1:]
    return values.at[tuple(spot)].set(least).at[tuple(beside)].set(top_value)


def levels(key, dims, shards, smallest, high):
    level, own = 1.0, jax.random.fold_in(key, 6)
    for dim, shards_of in shards:
        steps = jnp.exp(jax.random.uniform(jax.random.fold_in(own, dim), (shards_of,), jnp.float32, smallest / len(shards), high / len(shards)))
        level = level * jnp.repeat(steps, dims[dim] // shards_of).reshape([-1 if axis == dim else 1 for axis in range(len(dims))])
    return level


def bell_draw(key, extent, width, limit, cuts=(), kind=jnp.bfloat16):
    level = levels(key, extent, cuts, -0.22, 0.18) if cuts else 1.0
    values = jax.random.normal(key, extent, jnp.float32) * width * level
    return jnp.minimum(jnp.maximum(values, -limit), limit).astype(kind)


def setup_inputs(seed: int = 0) -> dict:
    seeds = jax.random.split(jax.random.key(seed), 9)
    return {
        "positions": draw_positions(jax.random.fold_in(seeds[8], 71), 0),
        "velocities": bell_draw(seeds[1], (3, NBEADS), 0.3, 2.5, ((1, 512),), jnp.float32),
        "bead_types": place_ends(jax.random.randint(seeds[2], (NBEADS,), 0, NTYPE), jax.random.fold_in(seeds[2], 1), 0, NTYPE - 1).astype(jnp.int32),
        "slot_bead": draw_slot_bead(jax.random.fold_in(seeds[8], 71), 0),
        "tile_pairs": draw_tile_pairs(jax.random.fold_in(seeds[8], 71), 0),
        "tile_count": draw_tile_count(jax.random.fold_in(seeds[8], 71), 0),
        "c6_table": draw_c6_table(jax.random.fold_in(seeds[8], 71), 0),
        "c12_table": draw_c12_table(jax.random.fold_in(seeds[8], 71), 0),
    }


SOFT_CORE = 0.25
CUT_OFF = 1.2
CELL_SIDE = 2.47
KICK_FACTOR = 0.02 / 72.0
HIGH = lax.Precision.HIGHEST


def pair_forces(i_beads, j_beads, i_table6, i_table12, j_onehot, live, j_keep, box_x, box_y):
    offset = i_beads[:, :, :, None] - j_beads[:, :, None, :]
    off_x = offset[0] - box_x * jnp.floor(offset[0] / box_x + 0.5)
    off_y = offset[1] - box_y * jnp.floor(offset[1] / box_y + 0.5)
    off_z = offset[2]
    dist_sq = off_x * off_x + off_y * off_y + off_z * off_z
    coef6 = jnp.einsum("kba,kbc->bac", i_table6, j_onehot, precision=HIGH)
    coef12 = jnp.einsum("kba,kbc->bac", i_table12, j_onehot, precision=HIGH)
    inverse = 1.0 / (dist_sq + SOFT_CORE)
    inverse3 = inverse * inverse * inverse
    cut_inv = 1.0 / (CUT_OFF * CUT_OFF + SOFT_CORE)
    cut3 = cut_inv * cut_inv * cut_inv
    scalar = (12.0 * coef12 * inverse3 * inverse3 - 6.0 * coef6 * inverse3) * inverse
    scalar = scalar - (12.0 * coef12 * cut3 * cut3 - 6.0 * coef6 * cut3) * cut_inv
    scalar = jnp.where(dist_sq < CUT_OFF * CUT_OFF, scalar, 0.0) * live[:, None, None]
    weighted = scalar[None] * jnp.stack([off_x, off_y, off_z])
    return jnp.sum(weighted, axis=3), -jnp.sum(weighted, axis=2) * j_keep[:, None]


def run_tiles(i_xyz, i_tab6, i_tab12, j_xyz, j_onehot, i_block, j_block, live, j_keep, box_x, box_y):
    total = i_block.shape[0]
    size = math.gcd(total, 8)
    items = tuple(a.reshape(total // size, size) for a in (i_block, j_block, live, j_keep))
    init = (jnp.zeros(i_xyz.shape, i_xyz.dtype), jnp.zeros(j_xyz.shape, j_xyz.dtype))

    def step(carry, item):
        i_sel, j_sel, alive, keep = item
        force_i, force_j = pair_forces(jnp.take(i_xyz, i_sel, axis=1), jnp.take(j_xyz, j_sel, axis=1),
                                       jnp.take(i_tab6, i_sel, axis=1), jnp.take(i_tab12, i_sel, axis=1),
                                       jnp.take(j_onehot, j_sel, axis=1), alive, keep, box_x, box_y)
        return (carry[0].at[:, i_sel].add(force_i), carry[1].at[:, j_sel].add(force_j)), None

    result, _ = lax.scan(step, init, items)
    return result


def reference(positions, velocities, bead_types, slot_bead, tile_pairs, tile_count, c6_table, c12_table):
    group = BPD * BLOCK
    box_x = N_COL * CELL_SIDE
    box_y = N_ROW * CELL_SIDE
    slots = jnp.arange(NBEADS, dtype=jnp.int32)
    bead_index = (slots // group) * group + slot_bead
    ordered = jnp.take(positions, bead_index, axis=1)
    kinds = jnp.take(bead_types, bead_index)
    onehot = (kinds[None, :] == jnp.arange(NTYPE, dtype=jnp.int32)[:, None]).astype(positions.dtype)
    table6 = jnp.dot(c6_table, onehot, precision=HIGH).reshape(NTYPE, -1, BLOCK)
    table12 = jnp.dot(c12_table, onehot, precision=HIGH).reshape(NTYPE, -1, BLOCK)
    xyz = ordered.reshape(3, -1, BLOCK)
    onehot_blocks = onehot.reshape(NTYPE, -1, BLOCK)
    entry = jnp.arange(TILES, dtype=jnp.int32)
    device = entry // P_DEV
    row_at = device // N_COL
    col_at = device % N_COL
    i_block = row_at * N_COL * BPD + tile_pairs[0]
    local_j = tile_pairs[1]
    j_block = ((local_j // BPD) * N_COL + col_at) * BPD + local_j % BPD
    alive = (entry - device * P_DEV) < jnp.take(tile_count, device)
    live = alive.astype(positions.dtype)
    j_keep = (alive & (i_block != j_block)).astype(positions.dtype)
    force_i, force_j = run_tiles(xyz, table6, table12, xyz, onehot_blocks, i_block, j_block, live, j_keep,
                                 box_x, box_y)
    force = (force_i + force_j).reshape(3, NBEADS)
    return velocities.at[:, bead_index].add(KICK_FACTOR * force)
```

```python
import functools

import jax
import jax.numpy as jnp
import numpy as np
from jax import lax
from jax.experimental import pallas as pl
from jax.experimental.pallas import tpu as pltpu
from jax.sharding import PartitionSpec as P

F32 = jnp.float32
BF16 = jnp.bfloat16
I32 = jnp.int32
MESH = pl.DeviceIdType.MESH
HIGH = lax.Precision.HIGHEST

BLOCK = 128
BPD = 4
GROUP = BPD * BLOCK
N_ROW = 32
N_COL = 16
NTYPE = 18
TYPE_PAD = 24
SOFT_CORE = 0.25
CUT_SQ = 1.2 * 1.2
CELL_SIDE = 2.47
KICK_FACTOR = 0.02 / 72.0

GRID = 2.46875
WRAP_X = float(np.float32(N_COL * CELL_SIDE) - np.float32(N_COL * GRID))
WRAP_Y = float(np.float32(N_ROW * CELL_SIDE) - np.float32(N_ROW * GRID))

CUT_X = float(np.float32(CUT_SQ + SOFT_CORE))
FEATURES = 32 + 2 * TYPE_PAD
LINK = GROUP + 2 * BLOCK
GROUPS = (
    (0, 0, 0, 256),
    (0, 1, 0, 256),
    (0, 2, 128, 256),
    (1, 1, 256, 384),
    (1, 2, 256, 512),
    (1, 3, 256, 512),
)
NT = (((1,), (1,)), ((), ()))


def iota(shape, dim):
    return lax.broadcasted_iota(I32, shape, dim)


def split3(x):
    high = x.astype(BF16).astype(F32)
    rest = x - high
    mid = rest.astype(BF16).astype(F32)
    return high, mid, rest - mid


def kernel(
    pos_ref, typ_ref, slot_ref, pair_ref, count_ref, c6_ref, c12_ref, out_ref,
    rec, perm, stage, pairs, tab, lhs_w, lhs_6, lhs_12, own_z, expand, acc,
    send_sem, recv_sem,
):
    row, col = lax.axis_index("row"), lax.axis_index("col")
    u = 2 * (col % 8) + col // 8
    v = 2 * (row % 16) + row // 16

    def device_at(e, f):
        to_u = (u + e + N_COL) % N_COL
        to_v = (v + f + N_ROW) % N_ROW
        return (to_v // 2 + to_v % 2 * 16, to_u // 2 + to_u % 2 * 8)

    around = [(e, f) for f in (-1, 0, 1) for e in (-1, 0, 1) if (e, f) != (0, 0)]

    def slot_of(e, f):
        return (f + 1) * 3 + e + 1

    barrier = pltpu.get_barrier_semaphore()
    for e, f in around:
        pl.semaphore_signal(barrier, inc=1, device_id=device_at(e, f), device_id_type=MESH)

    perm[...] = (iota((GROUP, GROUP), 0) == slot_ref[...]).astype(F32).astype(BF16)
    stage[...] = jnp.zeros_like(stage)
    stage[0:3, :] = pos_ref[...]
    stage[3:4, :] = typ_ref[...].astype(F32)
    which = iota((8, GROUP), 0)
    lane = iota((8, GROUP), 1)
    layer = lane // BLOCK
    half = GRID * 0.5
    origin = jnp.where(which == 0, u.astype(F32) * GRID + half, 0.0)
    origin = jnp.where(which == 1, v.astype(F32) * GRID + half, origin)
    parts = jnp.concatenate(split3(stage[...] - origin), axis=0).astype(BF16)
    moved = jnp.dot(parts, perm[...], preferred_element_type=F32)
    own = moved[0:8] + moved[8:16] + moved[16:24]
    own = own - jnp.where(which == 2, layer.astype(F32) * GRID + half, 0.0)
    rec[4, :, 0:GROUP] = own[0:4]

    pairs[...] = jnp.zeros_like(pairs)
    pairs[0:2, 0:72] = pair_ref[...]
    code = pairs[...]
    first, second = code[0:1], code[1:2]
    at_a = 2 * ((first >> 2) & 7) + (first >> 5)
    at_b = 2 * ((second >> 2) & 15) + (second >> 6)
    du = (at_a - u + 1) & (N_COL - 1)
    dv = (at_b - v + 1) & (N_ROW - 1)
    ka, kb = first & 3, second & 3
    live = iota((1, BLOCK), 1) < count_ref[0]
    eight = iota((8, BLOCK), 0)
    full = iota((BLOCK, BLOCK), 0)

    def table(layer_at, at):
        left = jnp.where((eight == layer_at) & live, 1.0, 0.0).astype(BF16)
        right = jnp.where(full == at, 1.0, 0.0).astype(BF16)
        return lax.dot_general(left, right, NT, preferred_element_type=F32)

    rec[4, :, GROUP : GROUP + BLOCK] = table(ka, du * 16 + dv * 4 + kb)[0:4]
    rec[4, :, GROUP + BLOCK : LINK] = table(kb, dv * 16 + du * 4 + ka)[0:4]

    pl.semaphore_wait(barrier, 8)
    copies = []
    for e, f in around:
        width = GROUP if e and f else LINK
        copy = pltpu.make_async_remote_copy(
            src_ref=rec.at[4, :, pl.ds(0, width)],
            dst_ref=rec.at[slot_of(-e, -f), :, pl.ds(0, width)],
            send_sem=send_sem.at[slot_of(e, f)],
            recv_sem=recv_sem.at[slot_of(-e, -f)],
            device_id=device_at(e, f),
            device_id_type=MESH,
        )
        copy.start()
        copies.append(copy)

    row4 = which & 3
    upper = which < 4
    own8 = jnp.concatenate([own[0:4], own[0:4]], axis=0)
    zeros = jnp.zeros((2 * TYPE_PAD, BLOCK), F32)
    for a, (p, k, _, _) in enumerate(GROUPS):
        at = slice(k * BLOCK, (k + 1) * BLOCK)
        pick, low = row4[:, at], upper[:, at]
        x = own8[:, at] + jnp.where(pick == 2, (k - 2 * p - 0.5) * GRID, 0.0)
        own_z[a] = x
        x = jnp.where(pick == 3, 0.0, x)
        norm = jnp.sum(x[0:4] * x[0:4], axis=0, keepdims=True) + SOFT_CORE
        h, m, l = split3(x)
        one = jnp.where(pick == 3, 1.0, 0.0)
        nh, nm, nl = split3(norm)
        kind = which[:, at]
        sides = [
            -2.0 * h + one,
            -2.0 * jnp.where(low, m, h) + jnp.where(low, 0.0, one),
            -2.0 * jnp.where(low, l, m),
            jnp.where(kind == 0, nh, jnp.where(kind == 1, nm, jnp.where(kind == 2, nl, 0.0))),
            zeros,
        ]
        lhs_w[a] = jnp.concatenate(sides, axis=0).T.astype(BF16)

    kinds = (iota((TYPE_PAD, GROUP), 0).astype(F32) == own[3:4]).astype(F32)
    blank = jnp.zeros((32, BLOCK), F32)
    for source, target, factor in ((c6_ref, lhs_6, 6.0), (c12_ref, lhs_12, 12.0)):
        tab[...] = jnp.zeros_like(tab)
        tab[0:NTYPE, 0:NTYPE] = source[...] * factor
        coef = jnp.dot(tab[:, 0:TYPE_PAD], kinds, precision=HIGH, preferred_element_type=F32)
        high = coef.astype(BF16).astype(F32)
        low = coef - high
        for k in range(BPD):
            at = slice(k * BLOCK, (k + 1) * BLOCK)
            side = jnp.concatenate([blank, high[:, at], low[:, at]], axis=0)
            target[k] = side.T.astype(BF16)
    expand[...] = (iota((16, GROUP), 0) == iota((16, GROUP), 1) // BLOCK).astype(F32).astype(BF16)
    acc[...] = jnp.zeros_like(acc)

    inv_cut = 1.0 / (CUT_X)
    cut4 = inv_cut**4
    cut7 = inv_cut**7

    def column(t, carry):
        corner = t // 5
        own_turn = (8 - t) // 8
        slot = (
            own_turn * 4
            + (1 - corner) * (1 - own_turn) * (2 * t - 1)
            + corner * (2 * (t - 5) + 2 * ((t + 1) // 2 - 3))
        )
        e, f = slot % 3 - 1, slot // 3 - 1

        @pl.when(t > 0)
        def _():
            @pl.when(t < 5)
            def _():
                pltpu.make_async_remote_copy(
                    src_ref=rec.at[4], dst_ref=rec.at[slot],
                    send_sem=send_sem.at[slot], recv_sem=recv_sem.at[slot],
                    device_id=device_at(e, f), device_id_type=MESH,
                ).wait_recv()

            @pl.when(t >= 5)
            def _():
                pltpu.make_async_remote_copy(
                    src_ref=rec.at[4, :, pl.ds(0, GROUP)],
                    dst_ref=rec.at[slot, :, pl.ds(0, GROUP)],
                    send_sem=send_sem.at[slot], recv_sem=recv_sem.at[slot],
                    device_id=device_at(e, f), device_id_type=MESH,
                ).wait_recv()

        tab_u = rec[3 + e + 1, :, GROUP : GROUP + BLOCK]
        tab_v = rec[(f + 1) * 3 + 1, :, GROUP + BLOCK : LINK]
        shift_u = BLOCK - ((1 - e) * 16 + (1 + f) * 4)
        shift_v = BLOCK - ((1 - f) * 16 + (1 + e) * 4)
        tab_u = pltpu.roll(jnp.concatenate([tab_u, tab_u], axis=0), shift_u, 1)
        tab_v = pltpu.roll(jnp.concatenate([tab_v, tab_v], axis=0), shift_v, 1)
        seen = (tab_u + tab_v)[:, 0:16]
        weight = jnp.dot(seen.astype(BF16), expand[...], preferred_element_type=F32)
        twice = jnp.where((slot == 4) & (which == layer), 0.5, 1.0)
        weight = weight * twice

        beads = rec[slot, :, 0:GROUP]
        beads = jnp.concatenate([beads, beads], axis=0)
        over_u = (u + e + N_COL) // N_COL - 1
        over_v = (v + f + N_ROW) // N_ROW - 1
        shift_x = e.astype(F32) * GRID + over_u.astype(F32) * WRAP_X
        shift_y = f.astype(F32) * GRID + over_v.astype(F32) * WRAP_Y
        shift_z = ((layer & 1).astype(F32) - 0.5) * GRID
        shift = jnp.where(row4 == 0, shift_x, jnp.where(row4 == 1, shift_y, shift_z))
        x = jnp.where(row4 == 3, 0.0, beads + shift)
        norm = jnp.sum(x[0:4] * x[0:4], axis=0, keepdims=True)
        h, m, l = split3(jnp.where(row4 == 3, norm, x))
        high_mid = jnp.where(upper, h, m)
        kind_row = iota((TYPE_PAD, GROUP), 0).astype(F32)
        onehot = (kind_row == beads[3:4]).astype(F32)
        rhs = jnp.concatenate(
            [high_mid, jnp.where(upper, h, l), high_mid, jnp.ones((8, GROUP), F32), onehot, onehot],
            axis=0,
        ).astype(BF16)
        back = jnp.concatenate([high_mid, jnp.where(upper, l, 1.0)], axis=0)

        for a, (p, k, start, stop) in enumerate(GROUPS):
            side = rhs[:, start:stop]
            dist = jnp.dot(lhs_w[a], side, preferred_element_type=F32)
            c6 = jnp.dot(lhs_6[k], side, preferred_element_type=F32)
            c12 = jnp.dot(lhs_12[k], side, preferred_element_type=F32)
            inv = 1.0 / jnp.minimum(dist, CUT_X)
            inv2 = inv * inv
            inv3 = inv2 * inv
            inv4 = inv2 * inv2
            scalar = c12 * (inv4 * inv3 - cut7) - c6 * (inv4 - cut4)
            high = scalar.astype(BF16)
            low = (scalar - high.astype(F32)).astype(BF16)
            pull = (back[:, start:stop] * weight[k : k + 1, start:stop]).astype(BF16)
            acc[a] += lax.dot_general(pull, high, NT, preferred_element_type=F32) + lax.dot_general(
                pull, low, NT, preferred_element_type=F32
            )
        return carry

    lax.fori_loop(0, 9, column, 0)

    force = []
    for k in range(BPD):
        total = jnp.zeros((8, BLOCK), F32)
        for a, group in enumerate(GROUPS):
            if group[1] == k:
                got = acc[a]
                pulled = got[0:8] + pltpu.roll(got[0:8], 4, 0) + got[8:16]
                total += own_z[a] * got[12:13] - pulled
        force.append(total)
    force = jnp.concatenate(force, axis=1) * KICK_FACTOR
    parts = jnp.concatenate(split3(force), axis=0).astype(BF16)
    stored = lax.dot_general(parts, perm[...], NT, preferred_element_type=F32)
    out_ref[...] = (stored[0:8] + stored[8:16] + stored[16:24])[0:3]

    for copy in copies:
        copy.wait_send()


def body(positions, velocities, bead_types, slot_bead, tile_pairs, tile_count, c6_table, c12_table):
    vmem = pl.BlockSpec(memory_space=pltpu.VMEM)
    smem = pl.BlockSpec(memory_space=pltpu.SMEM)
    kick = pl.pallas_call(
        kernel,
        out_shape=jax.ShapeDtypeStruct((3, GROUP), F32),
        in_specs=[vmem, vmem, vmem, vmem, smem, vmem, vmem],
        out_specs=vmem,
        scratch_shapes=[
            pltpu.VMEM((9, 4, LINK), F32),
            pltpu.VMEM((GROUP, GROUP), BF16),
            pltpu.VMEM((8, GROUP), F32),
            pltpu.VMEM((8, BLOCK), I32),
            pltpu.VMEM((TYPE_PAD, BLOCK), F32),
            pltpu.VMEM((6, BLOCK, FEATURES), BF16),
            pltpu.VMEM((4, BLOCK, FEATURES), BF16),
            pltpu.VMEM((4, BLOCK, FEATURES), BF16),
            pltpu.VMEM((6, 8, BLOCK), F32),
            pltpu.VMEM((16, GROUP), BF16),
            pltpu.VMEM((6, 16, BLOCK), F32),
            pltpu.SemaphoreType.DMA((9,)),
            pltpu.SemaphoreType.DMA((9,)),
        ],
        compiler_params=pltpu.CompilerParams(
            collective_id=0, has_side_effects=True, vmem_limit_bytes=48 * 2**20
        ),
        name="column_forces",
    )(
        positions,
        bead_types.reshape(1, GROUP),
        slot_bead.reshape(1, GROUP),
        tile_pairs,
        tile_count,
        c6_table,
        c12_table,
    )
    return velocities + kick


def solution(mesh):
    return jax.shard_map(
        body,
        mesh=mesh,
        in_specs=(
            P(None, ("row", "col")),
            P(None, ("row", "col")),
            P(("row", "col")),
            P(("row", "col")),
            P(None, ("row", "col")),
            P(("row", "col")),
            P(),
            P(),
        ),
        out_specs=P(None, ("row", "col")),
        check_vma=False,
    )
```

```python
import functools

import jax
import jax.numpy as jnp
import numpy as np
from jax import lax
from jax.experimental import pallas as pl
from jax.experimental.pallas import tpu as pltpu
from jax.sharding import PartitionSpec as P

F32 = jnp.float32
BF16 = jnp.bfloat16
I32 = jnp.int32
MESH = pl.DeviceIdType.MESH
HIGH = lax.Precision.HIGHEST

BLOCK = 128
BPD = 4
GROUP = BPD * BLOCK
N_ROW = 32
N_COL = 16
NTYPE = 18
TYPE_PAD = 24
SOFT_CORE = 0.25
CUT_SQ = 1.2 * 1.2
CELL_SIDE = 2.47
KICK_FACTOR = 0.02 / 72.0

GRID = 2.46875
WRAP_X = float(np.float32(N_COL * CELL_SIDE) - np.float32(N_COL * GRID))
WRAP_Y = float(np.float32(N_ROW * CELL_SIDE) - np.float32(N_ROW * GRID))

CUT_X = float(np.float32(CUT_SQ + SOFT_CORE))
FEATURES = 32 + 2 * TYPE_PAD
LINK = GROUP + 2 * BLOCK
GROUPS = (
    (0, 0, 256, 0, 256),
    (0, 256, 384, 128, 256),
    (1, 128, 256, 256, 384),
    (1, 256, 512, 256, 512),
)
CHUNK = 64
NT = (((1,), (1,)), ((), ()))


def iota(shape, dim):
    return lax.broadcasted_iota(I32, shape, dim)


def split3(x):
    high = x.astype(BF16).astype(F32)
    rest = x - high
    mid = rest.astype(BF16).astype(F32)
    return high, mid, rest - mid


def kernel(
    pos_hbm, typ_hbm, slot_hbm, pair_hbm, count_hbm, c6_hbm, c12_hbm, out_ref,
    pos_ref, typ_ref, slot_ref, pair_ref, count_ref, c6_ref, c12_ref,
    rec, perm, stage, pairs, tab, rhs_w, rhs_6, rhs_12, own_z, expand, feat, high, low, acc,
    load_sem, send_sem, recv_sem,
):
    loads = [
        pltpu.make_async_copy(source, target, load_sem.at[n])
        for n, (source, target) in enumerate((
            (slot_hbm, slot_ref), (pos_hbm, pos_ref), (typ_hbm, typ_ref), (pair_hbm, pair_ref),
            (count_hbm, count_ref), (c6_hbm, c6_ref), (c12_hbm, c12_ref),
        ))
    ]
    for load in loads:
        load.start()
    row, col = lax.axis_index("row"), lax.axis_index("col")
    u = 2 * (col % 8) + col // 8
    v = 2 * (row % 16) + row // 16

    def device_at(e, f):
        to_u = (u + e + N_COL) % N_COL
        to_v = (v + f + N_ROW) % N_ROW
        return (to_v // 2 + to_v % 2 * 16, to_u // 2 + to_u % 2 * 8)

    around = [(e, f) for f in (-1, 0, 1) for e in (-1, 0, 1) if (e, f) != (0, 0)]

    def slot_of(e, f):
        return (f + 1) * 3 + e + 1

    barrier = pltpu.get_barrier_semaphore()
    for e, f in around:
        pl.semaphore_signal(barrier, inc=1, device_id=device_at(e, f), device_id_type=MESH)

    for load in loads:
        load.wait()

    perm[...] = (iota((GROUP, GROUP), 0) == slot_ref[...]).astype(F32).astype(BF16)
    stage[...] = jnp.zeros_like(stage)
    stage[0:3, :] = pos_ref[...]
    stage[3:4, :] = typ_ref[...].astype(F32)
    which = iota((8, GROUP), 0)
    lane = iota((8, GROUP), 1)
    layer = lane // BLOCK
    half = GRID * 0.5
    origin = jnp.where(which == 0, u.astype(F32) * GRID + half, 0.0)
    origin = jnp.where(which == 1, v.astype(F32) * GRID + half, origin)
    parts = jnp.concatenate(split3(stage[...] - origin), axis=0).astype(BF16)
    moved = jnp.dot(parts, perm[...], preferred_element_type=F32)
    own = moved[0:8] + moved[8:16] + moved[16:24]
    own = own - jnp.where(which == 2, layer.astype(F32) * GRID + half, 0.0)
    rec[4, :, 0:GROUP] = own[0:4]

    pairs[...] = jnp.zeros_like(pairs)
    pairs[0:2, 0:72] = pair_ref[...]
    code = pairs[...]
    first, second = code[0:1], code[1:2]
    at_a = 2 * ((first >> 2) & 7) + (first >> 5)
    at_b = 2 * ((second >> 2) & 15) + (second >> 6)
    du = (at_a - u + 1) & (N_COL - 1)
    dv = (at_b - v + 1) & (N_ROW - 1)
    ka, kb = first & 3, second & 3
    live = iota((1, BLOCK), 1) < count_ref[0]
    eight = iota((8, BLOCK), 0)
    full = iota((BLOCK, BLOCK), 0)

    def table(layer_at, at):
        left = jnp.where((eight == layer_at) & live, 1.0, 0.0).astype(BF16)
        right = jnp.where(full == at, 1.0, 0.0).astype(BF16)
        return lax.dot_general(left, right, NT, preferred_element_type=F32)

    rec[4, :, GROUP : GROUP + BLOCK] = table(ka, du * 16 + dv * 4 + kb)[0:4]
    rec[4, :, GROUP + BLOCK : LINK] = table(kb, dv * 16 + du * 4 + ka)[0:4]

    pl.semaphore_wait(barrier, 8)
    copies = []
    for e, f in around:
        width = GROUP if e and f else LINK
        copy = pltpu.make_async_remote_copy(
            src_ref=rec.at[4, :, pl.ds(0, width)],
            dst_ref=rec.at[slot_of(-e, -f), :, pl.ds(0, width)],
            send_sem=send_sem.at[slot_of(e, f)],
            recv_sem=recv_sem.at[slot_of(-e, -f)],
            device_id=device_at(e, f),
            device_id_type=MESH,
        )
        copy.start()
        copies.append(copy)

    row4 = which & 3
    upper = which < 4
    own8 = jnp.concatenate([own[0:4], own[0:4]], axis=0)
    one = jnp.where(row4 == 3, 1.0, 0.0)
    zeros = jnp.zeros((2 * TYPE_PAD, GROUP), F32)
    for p in range(2):
        x = own8 + jnp.where(row4 == 2, (layer.astype(F32) - (2 * p + 0.5)) * GRID, 0.0)
        x = jnp.where(row4 == 3, 0.0, x)
        own_z[p] = x
        norm = jnp.sum(x[0:4] * x[0:4], axis=0, keepdims=True) + SOFT_CORE
        h, m, l = split3(x)
        nh, nm, nl = split3(norm)
        sides = [
            -2.0 * h + one,
            -2.0 * jnp.where(upper, m, h) + jnp.where(upper, 0.0, one),
            -2.0 * jnp.where(upper, l, m),
            jnp.where(which == 0, nh, jnp.where(which == 1, nm, jnp.where(which == 2, nl, 0.0))),
            zeros,
        ]
        rhs_w[p] = jnp.concatenate(sides, axis=0).astype(BF16)

    kinds = (iota((TYPE_PAD, GROUP), 0).astype(F32) == own[3:4]).astype(F32)
    blank = jnp.zeros((32, GROUP), F32)
    for source, target, factor in ((c6_ref, rhs_6, 6.0), (c12_ref, rhs_12, 12.0)):
        tab[...] = jnp.zeros_like(tab)
        tab[0:NTYPE, 0:NTYPE] = source[...] * factor
        coef = jnp.dot(tab[:, 0:TYPE_PAD], kinds, precision=HIGH, preferred_element_type=F32)
        first_part = coef.astype(BF16).astype(F32)
        target[...] = jnp.concatenate([blank, first_part, coef - first_part], axis=0).astype(BF16)
    expand[...] = (iota((16, GROUP), 0) == iota((16, GROUP), 1) // BLOCK).astype(F32).astype(BF16)
    acc[...] = jnp.zeros_like(acc)

    inv_cut = 1.0 / (CUT_X)
    cut4 = inv_cut**4
    cut7 = inv_cut**7

    ahead = 1 - 2 * (v % 2)

    def wait(slot, width):
        pltpu.make_async_remote_copy(
            src_ref=rec.at[4, :, pl.ds(0, width)],
            dst_ref=rec.at[slot, :, pl.ds(0, width)],
            send_sem=send_sem.at[slot], recv_sem=recv_sem.at[slot],
            device_id=device_at(1, 0), device_id_type=MESH,
        ).wait_recv()

    def features(slot, at, scale):
        e, f = slot % 3 - 1, slot // 3 - 1
        tab_u = rec[3 + e + 1, :, GROUP : GROUP + BLOCK]
        tab_v = rec[(f + 1) * 3 + 1, :, GROUP + BLOCK : LINK]
        shift_u = BLOCK - ((1 - e) * 16 + (1 + f) * 4)
        shift_v = BLOCK - ((1 - f) * 16 + (1 + e) * 4)
        tab_u = pltpu.roll(jnp.concatenate([tab_u, tab_u], axis=0), shift_u, 1)
        tab_v = pltpu.roll(jnp.concatenate([tab_v, tab_v], axis=0), shift_v, 1)
        seen = (tab_u + tab_v)[:, 0:16]
        weight = jnp.dot(seen.astype(BF16), expand[...], preferred_element_type=F32)
        twice = jnp.where((slot == 4) & (which == layer), 0.5, 1.0)
        weight = weight * twice * scale

        beads = rec[slot, :, 0:GROUP]
        beads = jnp.concatenate([beads, beads], axis=0)
        over_u = (u + e + N_COL) // N_COL - 1
        over_v = (v + f + N_ROW) // N_ROW - 1
        shift_x = e.astype(F32) * GRID + over_u.astype(F32) * WRAP_X
        shift_y = f.astype(F32) * GRID + over_v.astype(F32) * WRAP_Y
        shift_z = ((layer & 1).astype(F32) - 0.5) * GRID
        shift = jnp.where(row4 == 0, shift_x, jnp.where(row4 == 1, shift_y, shift_z))
        x = jnp.where(row4 == 3, 0.0, beads + shift)
        norm = jnp.sum(x[0:4] * x[0:4], axis=0, keepdims=True)
        h, m, l = split3(jnp.where(row4 == 3, norm, x))
        high_mid = jnp.where(upper, h, m)
        kind_row = iota((TYPE_PAD, GROUP), 0).astype(F32)
        onehot = (kind_row == beads[3:4]).astype(F32)
        rows = jnp.concatenate(
            [high_mid, jnp.where(upper, h, l), high_mid, jnp.ones((8, GROUP), F32), onehot, onehot],
            axis=0,
        )
        for k in range(BPD):
            feat[at, k * BLOCK : (k + 1) * BLOCK, :] = rows[:, k * BLOCK : (k + 1) * BLOCK].T.astype(BF16)
        back = jnp.concatenate([high_mid, jnp.where(upper, l, 1.0)], axis=0)
        return back, weight

    def scalars(at):
        for p, m0, m1, n0, n1 in GROUPS:
            for n in range(n0, n1, CHUNK):
                side = feat[at, n : n + CHUNK, :]
                dist = jnp.dot(side, rhs_w[p, :, m0:m1], preferred_element_type=F32)
                c6 = jnp.dot(side, rhs_6[:, m0:m1], preferred_element_type=F32)
                c12 = jnp.dot(side, rhs_12[:, m0:m1], preferred_element_type=F32)
                inv = 1.0 / jnp.minimum(dist, CUT_X)
                inv2 = inv * inv
                inv3 = inv2 * inv
                inv4 = inv2 * inv2
                scalar = c12 * (inv4 * inv3 - cut7) - c6 * (inv4 - cut4)
                rounded = scalar.astype(BF16)
                high[at, n : n + CHUNK, m0:m1] = rounded
                low[at, n : n + CHUNK, m0:m1] = (scalar - rounded.astype(F32)).astype(BF16)

    def sums(at, back, weight):
        for p, m0, m1, n0, n1 in GROUPS:
            layers = range(m0 // BLOCK, m1 // BLOCK)
            pull = jnp.concatenate(
                [back[:, n0:n1] * weight[k : k + 1, n0:n1] for k in layers], axis=0
            ).astype(BF16)
            got = jnp.dot(pull, high[at, n0:n1, m0:m1], preferred_element_type=F32) + jnp.dot(
                pull, low[at, n0:n1, m0:m1], preferred_element_type=F32
            )
            for n, k in enumerate(layers):
                lanes = slice(k * BLOCK, (k + 1) * BLOCK)
                acc[p, :, lanes] += got[16 * n : 16 * n + 16, n * BLOCK : (n + 1) * BLOCK]

    def two_columns(t, carry):
        is_u = (t == 1).astype(I32)
        is_far = (t == 2).astype(I32)
        is_side = (t == 3).astype(I32)
        is_near = (t == 4).astype(I32)
        e = is_u + is_far + is_near
        f = is_far * ahead - is_near * ahead
        one_slot = (f + is_side * ahead + 1) * 3 + 1 - e
        two_slot = (f - is_side * ahead + 1) * 3 + 1 + e

        @pl.when(is_u == 1)
        def _():
            wait(one_slot, LINK)
            wait(two_slot, LINK)

        @pl.when(is_far == 1)
        def _():
            wait((ahead + 1) * 3 + 1, LINK)

        @pl.when(is_side == 1)
        def _():
            wait((1 - ahead) * 3 + 1, LINK)

        @pl.when(is_far + is_near == 1)
        def _():
            wait(one_slot, GROUP)
            wait(two_slot, GROUP)

        scale = jnp.minimum(t, 1).astype(F32)
        first_side = features(one_slot, 0, 1.0)
        second_side = features(two_slot, 1, scale)
        scalars(0)
        scalars(1)
        sums(0, *first_side)
        sums(1, *second_side)
        return carry

    lax.fori_loop(0, 5, two_columns, 0)

    force = jnp.zeros((8, GROUP), F32)
    for p in range(2):
        got = acc[p]
        pulled = got[0:8] + pltpu.roll(got[0:8], 4, 0) + got[8:16]
        force += own_z[p] * got[12:13] - pulled
    force = force * KICK_FACTOR
    parts = jnp.concatenate(split3(force), axis=0).astype(BF16)
    stored = lax.dot_general(parts, perm[...], NT, preferred_element_type=F32)
    out_ref[...] = (stored[0:8] + stored[8:16] + stored[16:24])[0:3]

    for copy in copies:
        copy.wait_send()


def body(positions, velocities, bead_types, slot_bead, tile_pairs, tile_count, c6_table, c12_table):
    vmem = pl.BlockSpec(memory_space=pltpu.VMEM)
    hbm = pl.BlockSpec(memory_space=pltpu.HBM)
    kick = pl.pallas_call(
        kernel,
        out_shape=jax.ShapeDtypeStruct((3, GROUP), F32),
        in_specs=[hbm] * 7,
        out_specs=vmem,
        scratch_shapes=[
            pltpu.VMEM((3, GROUP), F32),
            pltpu.VMEM((1, GROUP), I32),
            pltpu.VMEM((1, GROUP), I32),
            pltpu.VMEM((2, 72), I32),
            pltpu.SMEM((1,), I32),
            pltpu.VMEM((NTYPE, NTYPE), F32),
            pltpu.VMEM((NTYPE, NTYPE), F32),
            pltpu.VMEM((9, 4, LINK), F32),
            pltpu.VMEM((GROUP, GROUP), BF16),
            pltpu.VMEM((8, GROUP), F32),
            pltpu.VMEM((8, BLOCK), I32),
            pltpu.VMEM((TYPE_PAD, BLOCK), F32),
            pltpu.VMEM((2, FEATURES, GROUP), BF16),
            pltpu.VMEM((FEATURES, GROUP), BF16),
            pltpu.VMEM((FEATURES, GROUP), BF16),
            pltpu.VMEM((2, 8, GROUP), F32),
            pltpu.VMEM((16, GROUP), BF16),
            pltpu.VMEM((2, GROUP, FEATURES), BF16),
            pltpu.VMEM((2, GROUP, GROUP), BF16),
            pltpu.VMEM((2, GROUP, GROUP), BF16),
            pltpu.VMEM((2, 16, GROUP), F32),
            pltpu.SemaphoreType.DMA((7,)),
            pltpu.SemaphoreType.DMA((9,)),
            pltpu.SemaphoreType.DMA((9,)),
        ],
        compiler_params=pltpu.CompilerParams(
            collective_id=0, has_side_effects=True, vmem_limit_bytes=60 * 2**20
        ),
        name="column_forces",
    )(
        positions,
        bead_types.reshape(1, GROUP),
        slot_bead.reshape(1, GROUP),
        tile_pairs,
        tile_count,
        c6_table,
        c12_table,
    )
    return velocities + kick


def solution(mesh):
    return jax.shard_map(
        body,
        mesh=mesh,
        in_specs=(
            P(None, ("row", "col")),
            P(None, ("row", "col")),
            P(("row", "col")),
            P(("row", "col")),
            P(None, ("row", "col")),
            P(("row", "col")),
            P(),
            P(),
        ),
        out_specs=P(None, ("row", "col")),
        check_vma=False,
    )
```

```python
import functools

import jax
import jax.numpy as jnp
import numpy as np
from jax import lax
from jax.experimental import pallas as pl
from jax.experimental.pallas import tpu as pltpu
from jax.sharding import PartitionSpec as P

F32 = jnp.float32
BF16 = jnp.bfloat16
I32 = jnp.int32
MESH = pl.DeviceIdType.MESH
HIGH = lax.Precision.HIGHEST

BLOCK = 128
BPD = 4
GROUP = BPD * BLOCK
N_ROW = 32
N_COL = 16
NTYPE = 18
TYPE_PAD = 24
SOFT_CORE = 0.25
CUT_SQ = 1.2 * 1.2
CELL_SIDE = 2.47
KICK_FACTOR = 0.02 / 72.0

GRID = 2.46875
WRAP_X = float(np.float32(N_COL * CELL_SIDE) - np.float32(N_COL * GRID))
WRAP_Y = float(np.float32(N_ROW * CELL_SIDE) - np.float32(N_ROW * GRID))

CUT_X = float(np.float32(CUT_SQ + SOFT_CORE))
FEATURES = 32 + 2 * TYPE_PAD
LINK = GROUP + 2 * BLOCK
GROUPS = (
    (0, 0, 256, 0, 256),
    (0, 256, 384, 128, 256),
    (1, 128, 256, 256, 384),
    (1, 256, 512, 256, 512),
)
CHUNK = 64
NT = (((1,), (1,)), ((), ()))


def iota(shape, dim):
    return lax.broadcasted_iota(I32, shape, dim)


def split3(x):
    high = x.astype(BF16).astype(F32)
    rest = x - high
    mid = rest.astype(BF16).astype(F32)
    return high, mid, rest - mid


def kernel(
    pos_hbm, typ_hbm, slot_hbm, pair_hbm, count_hbm, c6_hbm, c12_hbm, out_ref,
    pos_ref, typ_ref, slot_ref, pair_ref, count_ref, c6_ref, c12_ref,
    rec, perm, stage, pairs, tab, rhs_w, rhs_6, rhs_12, own_z, expand, feat, high, low, acc,
    load_sem, send_sem, recv_sem,
):
    loads = [
        pltpu.make_async_copy(source, target, load_sem.at[n])
        for n, (source, target) in enumerate((
            (slot_hbm, slot_ref), (pos_hbm, pos_ref), (typ_hbm, typ_ref), (pair_hbm, pair_ref),
            (count_hbm, count_ref), (c6_hbm, c6_ref), (c12_hbm, c12_ref),
        ))
    ]
    for load in loads:
        load.start()
    row, col = lax.axis_index("row"), lax.axis_index("col")
    u = 2 * (col % 8) + col // 8
    v = 2 * (row % 16) + row // 16

    def device_at(e, f):
        to_u = (u + e + N_COL) % N_COL
        to_v = (v + f + N_ROW) % N_ROW
        return (to_v // 2 + to_v % 2 * 16, to_u // 2 + to_u % 2 * 8)

    around = [(e, f) for f in (-1, 0, 1) for e in (-1, 0, 1) if (e, f) != (0, 0)]

    def slot_of(e, f):
        return (f + 1) * 3 + e + 1

    early = v % 16 == 0
    late = v % 16 == 15
    barrier = pltpu.get_barrier_semaphore()

    def greet(e, f):
        pl.semaphore_signal(barrier, inc=1, device_id=device_at(e, f), device_id_type=MESH)

    for e, f in around:
        if f < 1:
            greet(e, f)

    @pl.when(jnp.logical_not(late))
    def _():
        for e in (-1, 0, 1):
            greet(e, 1)

    for load in loads:
        load.wait()

    perm[...] = (iota((GROUP, GROUP), 0) == slot_ref[...]).astype(F32).astype(BF16)
    stage[...] = jnp.zeros_like(stage)
    stage[0:3, :] = pos_ref[...]
    stage[3:4, :] = typ_ref[...].astype(F32)
    which = iota((8, GROUP), 0)
    lane = iota((8, GROUP), 1)
    layer = lane // BLOCK
    half = GRID * 0.5
    origin = jnp.where(which == 0, u.astype(F32) * GRID + half, 0.0)
    origin = jnp.where(which == 1, v.astype(F32) * GRID + half, origin)
    parts = jnp.concatenate(split3(stage[...] - origin), axis=0).astype(BF16)
    moved = jnp.dot(parts, perm[...], preferred_element_type=F32)
    own = moved[0:8] + moved[8:16] + moved[16:24]
    own = own - jnp.where(which == 2, layer.astype(F32) * GRID + half, 0.0)
    rec[4, :, 0:GROUP] = own[0:4]

    pairs[...] = jnp.zeros_like(pairs)
    pairs[0:2, 0:72] = pair_ref[...]
    code = pairs[...]
    first, second = code[0:1], code[1:2]
    at_a = 2 * ((first >> 2) & 7) + (first >> 5)
    at_b = 2 * ((second >> 2) & 15) + (second >> 6)
    du = (at_a - u + 1) & (N_COL - 1)
    dv = (at_b - v + 1) & (N_ROW - 1)
    ka, kb = first & 3, second & 3
    live = iota((1, BLOCK), 1) < count_ref[0]
    eight = iota((8, BLOCK), 0)
    full = iota((BLOCK, BLOCK), 0)

    def table(layer_at, at):
        left = jnp.where((eight == layer_at) & live, 1.0, 0.0).astype(BF16)
        right = jnp.where(full == at, 1.0, 0.0).astype(BF16)
        return lax.dot_general(left, right, NT, preferred_element_type=F32)

    rec[4, :, GROUP : GROUP + BLOCK] = table(ka, du * 16 + dv * 4 + kb)[0:4]
    rec[4, :, GROUP + BLOCK : LINK] = table(kb, dv * 16 + du * 4 + ka)[0:4]

    def link(e, f):
        width = GROUP if e and f else LINK
        return pltpu.make_async_remote_copy(
            src_ref=rec.at[4, :, pl.ds(0, width)],
            dst_ref=rec.at[slot_of(-e, -f), :, pl.ds(0, width)],
            send_sem=send_sem.at[slot_of(e, f)],
            recv_sem=recv_sem.at[slot_of(-e, -f)],
            device_id=device_at(e, f),
            device_id_type=MESH,
        )

    @pl.when(early)
    def _():
        pl.semaphore_wait(barrier, 5)

    @pl.when(jnp.logical_not(early))
    def _():
        pl.semaphore_wait(barrier, 8)
        for e in (-1, 0, 1):
            link(e, -1).start()

    for e, f in around:
        if f > -1:
            link(e, f).start()

    row4 = which & 3
    upper = which < 4
    own8 = jnp.concatenate([own[0:4], own[0:4]], axis=0)
    one = jnp.where(row4 == 3, 1.0, 0.0)
    zeros = jnp.zeros((2 * TYPE_PAD, GROUP), F32)
    for p in range(2):
        x = own8 + jnp.where(row4 == 2, (layer.astype(F32) - (2 * p + 0.5)) * GRID, 0.0)
        x = jnp.where(row4 == 3, 0.0, x)
        own_z[p] = x
        norm = jnp.sum(x[0:4] * x[0:4], axis=0, keepdims=True) + SOFT_CORE
        h, m, l = split3(x)
        nh, nm, nl = split3(norm)
        sides = [
            -2.0 * h + one,
            -2.0 * jnp.where(upper, m, h) + jnp.where(upper, 0.0, one),
            -2.0 * jnp.where(upper, l, m),
            jnp.where(which == 0, nh, jnp.where(which == 1, nm, jnp.where(which == 2, nl, 0.0))),
            zeros,
        ]
        rhs_w[p] = jnp.concatenate(sides, axis=0).astype(BF16)

    kinds = (iota((TYPE_PAD, GROUP), 0).astype(F32) == own[3:4]).astype(F32)
    blank = jnp.zeros((32, GROUP), F32)
    for source, target, factor in ((c6_ref, rhs_6, 6.0), (c12_ref, rhs_12, 12.0)):
        tab[...] = jnp.zeros_like(tab)
        tab[0:NTYPE, 0:NTYPE] = source[...] * factor
        coef = jnp.dot(tab[:, 0:TYPE_PAD], kinds, precision=HIGH, preferred_element_type=F32)
        first_part = coef.astype(BF16).astype(F32)
        target[...] = jnp.concatenate([blank, first_part, coef - first_part], axis=0).astype(BF16)
    expand[...] = (iota((16, GROUP), 0) == iota((16, GROUP), 1) // BLOCK).astype(F32).astype(BF16)
    acc[...] = jnp.zeros_like(acc)

    inv_cut = 1.0 / (CUT_X)
    cut4 = inv_cut**4
    cut7 = inv_cut**7

    ahead = 1 - 2 * (v % 2)

    def wait(slot, width):
        pltpu.make_async_remote_copy(
            src_ref=rec.at[4, :, pl.ds(0, width)],
            dst_ref=rec.at[slot, :, pl.ds(0, width)],
            send_sem=send_sem.at[slot], recv_sem=recv_sem.at[slot],
            device_id=device_at(1, 0), device_id_type=MESH,
        ).wait_recv()

    def features(slot, at, scale):
        e, f = slot % 3 - 1, slot // 3 - 1
        tab_u = rec[3 + e + 1, :, GROUP : GROUP + BLOCK]
        tab_v = rec[(f + 1) * 3 + 1, :, GROUP + BLOCK : LINK]
        shift_u = BLOCK - ((1 - e) * 16 + (1 + f) * 4)
        shift_v = BLOCK - ((1 - f) * 16 + (1 + e) * 4)
        tab_u = pltpu.roll(jnp.concatenate([tab_u, tab_u], axis=0), shift_u, 1)
        tab_v = pltpu.roll(jnp.concatenate([tab_v, tab_v], axis=0), shift_v, 1)
        seen = (tab_u + tab_v)[:, 0:16]
        weight = jnp.dot(seen.astype(BF16), expand[...], preferred_element_type=F32)
        twice = jnp.where((slot == 4) & (which == layer), 0.5, 1.0)
        weight = weight * twice * scale

        beads = rec[slot, :, 0:GROUP]
        beads = jnp.concatenate([beads, beads], axis=0)
        over_u = (u + e + N_COL) // N_COL - 1
        over_v = (v + f + N_ROW) // N_ROW - 1
        shift_x = e.astype(F32) * GRID + over_u.astype(F32) * WRAP_X
        shift_y = f.astype(F32) * GRID + over_v.astype(F32) * WRAP_Y
        shift_z = ((layer & 1).astype(F32) - 0.5) * GRID
        shift = jnp.where(row4 == 0, shift_x, jnp.where(row4 == 1, shift_y, shift_z))
        x = jnp.where(row4 == 3, 0.0, beads + shift)
        norm = jnp.sum(x[0:4] * x[0:4], axis=0, keepdims=True)
        h, m, l = split3(jnp.where(row4 == 3, norm, x))
        high_mid = jnp.where(upper, h, m)
        kind_row = iota((TYPE_PAD, GROUP), 0).astype(F32)
        onehot = (kind_row == beads[3:4]).astype(F32)
        rows = jnp.concatenate(
            [high_mid, jnp.where(upper, h, l), high_mid, jnp.ones((8, GROUP), F32), onehot, onehot],
            axis=0,
        )
        for k in range(BPD):
            feat[at, k * BLOCK : (k + 1) * BLOCK, :] = rows[:, k * BLOCK : (k + 1) * BLOCK].T.astype(BF16)
        back = jnp.concatenate([high_mid, jnp.where(upper, l, 1.0)], axis=0)
        return back, weight

    def scalars(at):
        for p, m0, m1, n0, n1 in GROUPS:
            for n in range(n0, n1, CHUNK):
                side = feat[at, n : n + CHUNK, :]
                dist = jnp.dot(side, rhs_w[p, :, m0:m1], preferred_element_type=F32)
                c6 = jnp.dot(side, rhs_6[:, m0:m1], preferred_element_type=F32)
                c12 = jnp.dot(side, rhs_12[:, m0:m1], preferred_element_type=F32)
                inv = 1.0 / jnp.minimum(dist, CUT_X)
                inv2 = inv * inv
                inv3 = inv2 * inv
                inv4 = inv2 * inv2
                scalar = c12 * (inv4 * inv3 - cut7) - c6 * (inv4 - cut4)
                rounded = scalar.astype(BF16)
                high[at, n : n + CHUNK, m0:m1] = rounded
                low[at, n : n + CHUNK, m0:m1] = (scalar - rounded.astype(F32)).astype(BF16)

    def sums(at, back, weight):
        for p, m0, m1, n0, n1 in GROUPS:
            layers = range(m0 // BLOCK, m1 // BLOCK)
            pull = jnp.concatenate(
                [back[:, n0:n1] * weight[k : k + 1, n0:n1] for k in layers], axis=0
            ).astype(BF16)
            got = jnp.dot(pull, high[at, n0:n1, m0:m1], preferred_element_type=F32) + jnp.dot(
                pull, low[at, n0:n1, m0:m1], preferred_element_type=F32
            )
            for n, k in enumerate(layers):
                lanes = slice(k * BLOCK, (k + 1) * BLOCK)
                acc[p, :, lanes] += got[16 * n : 16 * n + 16, n * BLOCK : (n + 1) * BLOCK]

    def two_columns(t, carry):
        is_u = (t == 1).astype(I32)
        is_far = (t == 2).astype(I32)
        is_side = (t == 3).astype(I32)
        is_near = (t == 4).astype(I32)
        e = is_u + is_far + is_near
        f = is_far * ahead - is_near * ahead
        one_slot = (f + is_side * ahead + 1) * 3 + 1 - e
        two_slot = (f - is_side * ahead + 1) * 3 + 1 + e

        @pl.when(is_u == 1)
        def _():
            wait(one_slot, LINK)
            wait(two_slot, LINK)

        @pl.when(is_far == 1)
        def _():
            wait((ahead + 1) * 3 + 1, LINK)

        @pl.when(is_side == 1)
        def _():
            wait((1 - ahead) * 3 + 1, LINK)

            @pl.when(early)
            def _():
                link(0, -1).start()

        @pl.when(is_far + is_near == 1)
        def _():
            wait(one_slot, GROUP)
            wait(two_slot, GROUP)

        @pl.when((is_near == 1) & early)
        def _():
            link(-1, -1).start()
            link(1, -1).start()

        scale = jnp.minimum(t, 1).astype(F32)
        first_side = features(one_slot, 0, 1.0)
        second_side = features(two_slot, 1, scale)
        scalars(0)
        scalars(1)
        sums(0, *first_side)
        sums(1, *second_side)
        return carry

    lax.fori_loop(0, 5, two_columns, 0)

    force = jnp.zeros((8, GROUP), F32)
    for p in range(2):
        got = acc[p]
        pulled = got[0:8] + pltpu.roll(got[0:8], 4, 0) + got[8:16]
        force += own_z[p] * got[12:13] - pulled
    force = force * KICK_FACTOR
    parts = jnp.concatenate(split3(force), axis=0).astype(BF16)
    stored = lax.dot_general(parts, perm[...], NT, preferred_element_type=F32)
    out_ref[...] = (stored[0:8] + stored[8:16] + stored[16:24])[0:3]

    for e, f in around:
        link(e, f).wait_send()


def body(positions, velocities, bead_types, slot_bead, tile_pairs, tile_count, c6_table, c12_table):
    vmem = pl.BlockSpec(memory_space=pltpu.VMEM)
    hbm = pl.BlockSpec(memory_space=pltpu.HBM)
    kick = pl.pallas_call(
        kernel,
        out_shape=pltpu.VMEM((3, GROUP), F32),
        in_specs=[hbm] * 7,
        out_specs=vmem,
        scratch_shapes=[
            pltpu.VMEM((3, GROUP), F32),
            pltpu.VMEM((1, GROUP), I32),
            pltpu.VMEM((1, GROUP), I32),
            pltpu.VMEM((2, 72), I32),
            pltpu.SMEM((1,), I32),
            pltpu.VMEM((NTYPE, NTYPE), F32),
            pltpu.VMEM((NTYPE, NTYPE), F32),
            pltpu.VMEM((9, 4, LINK), F32),
            pltpu.VMEM((GROUP, GROUP), BF16),
            pltpu.VMEM((8, GROUP), F32),
            pltpu.VMEM((8, BLOCK), I32),
            pltpu.VMEM((TYPE_PAD, BLOCK), F32),
            pltpu.VMEM((2, FEATURES, GROUP), BF16),
            pltpu.VMEM((FEATURES, GROUP), BF16),
            pltpu.VMEM((FEATURES, GROUP), BF16),
            pltpu.VMEM((2, 8, GROUP), F32),
            pltpu.VMEM((16, GROUP), BF16),
            pltpu.VMEM((2, GROUP, FEATURES), BF16),
            pltpu.VMEM((2, GROUP, GROUP), BF16),
            pltpu.VMEM((2, GROUP, GROUP), BF16),
            pltpu.VMEM((2, 16, GROUP), F32),
            pltpu.SemaphoreType.DMA((7,)),
            pltpu.SemaphoreType.DMA((9,)),
            pltpu.SemaphoreType.DMA((9,)),
        ],
        compiler_params=pltpu.CompilerParams(
            collective_id=0, has_side_effects=True, vmem_limit_bytes=60 * 2**20
        ),
        name="column_forces",
    )(
        positions,
        bead_types.reshape(1, GROUP),
        slot_bead.reshape(1, GROUP),
        tile_pairs,
        tile_count,
        c6_table,
        c12_table,
    )
    return velocities + kick


def solution(mesh):
    return jax.shard_map(
        body,
        mesh=mesh,
        in_specs=(
            P(None, ("row", "col")),
            P(None, ("row", "col")),
            P(("row", "col")),
            P(("row", "col")),
            P(None, ("row", "col")),
            P(("row", "col")),
            P(),
            P(),
        ),
        out_specs=P(None, ("row", "col")),
        check_vma=False,
    )
```

```python
import functools

import jax
import jax.numpy as jnp
import numpy as np
from jax import lax
from jax.experimental import pallas as pl
from jax.experimental.pallas import tpu as pltpu
from jax.sharding import PartitionSpec as P

F32 = jnp.float32
BF16 = jnp.bfloat16
I32 = jnp.int32
MESH = pl.DeviceIdType.MESH
HIGH = lax.Precision.HIGHEST

BLOCK = 128
BPD = 4
GROUP = BPD * BLOCK
N_ROW = 32
N_COL = 16
NTYPE = 18
TYPE_PAD = 24
SOFT_CORE = 0.25
CUT_SQ = 1.2 * 1.2
CELL_SIDE = 2.47
KICK_FACTOR = 0.02 / 72.0

GRID = 2.46875
WRAP_X = float(np.float32(N_COL * CELL_SIDE) - np.float32(N_COL * GRID))
WRAP_Y = float(np.float32(N_ROW * CELL_SIDE) - np.float32(N_ROW * GRID))

CUT_X = float(np.float32(CUT_SQ + SOFT_CORE))
FEATURES = 32 + 2 * TYPE_PAD
LINK = GROUP + 2 * BLOCK
GROUPS = (
    (0, 0, 256, 0, 256),
    (0, 256, 384, 128, 256),
    (1, 128, 256, 256, 384),
    (1, 256, 512, 256, 512),
)
CHUNK = 64
NT = (((1,), (1,)), ((), ()))


def iota(shape, dim):
    return lax.broadcasted_iota(I32, shape, dim)


def split3(x):
    high = x.astype(BF16).astype(F32)
    rest = x - high
    mid = rest.astype(BF16).astype(F32)
    return high, mid, rest - mid


def kernel(
    pos_hbm, typ_hbm, slot_hbm, pair_hbm, count_hbm, c6_hbm, c12_hbm, out_ref,
    pos_ref, typ_ref, slot_ref, pair_ref, count_ref, c6_ref, c12_ref,
    rec, perm, unperm, stage, pairs, tab, rhs_w, rhs_6, rhs_12, own_z, expand, feat, high, low, acc,
    load_sem, send_sem, recv_sem,
):
    row, col = lax.axis_index("row"), lax.axis_index("col")
    u = 2 * (col % 8) + col // 8
    v = 2 * (row % 16) + row // 16

    def device_at(e, f):
        to_u = (u + e + N_COL) % N_COL
        to_v = (v + f + N_ROW) % N_ROW
        return (to_v // 2 + to_v % 2 * 16, to_u // 2 + to_u % 2 * 8)

    around = [(e, f) for f in (-1, 0, 1) for e in (-1, 0, 1) if (e, f) != (0, 0)]

    def slot_of(e, f):
        return (f + 1) * 3 + e + 1

    early = v % 16 == 0
    late = v % 16 == 15
    below = v % 16 == 14
    lower = v % 16 == 13
    late_odd = late & (u % 2 == 1)
    barrier = pltpu.get_barrier_semaphore()

    def greet(e, f):
        pl.semaphore_signal(barrier, inc=1, device_id=device_at(e, f), device_id_type=MESH)

    greet(0, -1)

    @pl.when(jnp.logical_not(late))
    def _():
        greet(-1, -1)
        greet(1, -1)

    @pl.when(jnp.logical_not(late | below))
    def _():
        greet(0, 1)

    @pl.when(jnp.logical_not(late | below | lower))
    def _():
        greet(-1, 1)
        greet(1, 1)

    @pl.when(jnp.logical_not(late & (u % 2 == 0)))
    def _():
        greet(-1, 0)
        greet(1, 0)

    loads = [
        pltpu.make_async_copy(source, target, load_sem.at[n])
        for n, (source, target) in enumerate((
            (slot_hbm, slot_ref), (pos_hbm, pos_ref), (typ_hbm, typ_ref), (pair_hbm, pair_ref),
            (count_hbm, count_ref), (c6_hbm, c6_ref), (c12_hbm, c12_ref),
        ))
    ]
    for load in loads:
        load.start()
    for load in loads:
        load.wait()

    perm[...] = (iota((GROUP, GROUP), 0) == slot_ref[...]).astype(F32).astype(BF16)
    stage[...] = jnp.zeros_like(stage)
    stage[0:3, :] = pos_ref[...]
    stage[3:4, :] = typ_ref[...].astype(F32)
    which = iota((8, GROUP), 0)
    lane = iota((8, GROUP), 1)
    layer = lane // BLOCK
    half = GRID * 0.5
    origin = jnp.where(which == 0, u.astype(F32) * GRID + half, 0.0)
    origin = jnp.where(which == 1, v.astype(F32) * GRID + half, origin)
    parts = jnp.concatenate(split3(stage[...] - origin), axis=0).astype(BF16)
    moved = jnp.dot(parts, perm[...], preferred_element_type=F32)
    own = moved[0:8] + moved[8:16] + moved[16:24]
    own = own - jnp.where(which == 2, layer.astype(F32) * GRID + half, 0.0)
    rec[4, :, 0:GROUP] = own[0:4]

    pairs[...] = jnp.zeros_like(pairs)
    pairs[0:2, 0:72] = pair_ref[...]
    code = pairs[...]
    first, second = code[0:1], code[1:2]
    at_a = 2 * ((first >> 2) & 7) + (first >> 5)
    at_b = 2 * ((second >> 2) & 15) + (second >> 6)
    du = (at_a - u + 1) & (N_COL - 1)
    dv = (at_b - v + 1) & (N_ROW - 1)
    ka, kb = first & 3, second & 3
    live = iota((1, BLOCK), 1) < count_ref[0]
    eight = iota((8, BLOCK), 0)
    full = iota((BLOCK, BLOCK), 0)

    def table(layer_at, at):
        left = jnp.where((eight == layer_at) & live, 1.0, 0.0).astype(BF16)
        right = jnp.where(full == at, 1.0, 0.0).astype(BF16)
        return lax.dot_general(left, right, NT, preferred_element_type=F32)

    rec[4, :, GROUP : GROUP + BLOCK] = table(ka, du * 16 + dv * 4 + kb)[0:4]
    rec[4, :, GROUP + BLOCK : LINK] = table(kb, dv * 16 + du * 4 + ka)[0:4]

    def link(e, f):
        width = GROUP if e and f else LINK
        return pltpu.make_async_remote_copy(
            src_ref=rec.at[4, :, pl.ds(0, width)],
            dst_ref=rec.at[slot_of(-e, -f), :, pl.ds(0, width)],
            send_sem=send_sem.at[slot_of(e, f)],
            recv_sem=recv_sem.at[slot_of(-e, -f)],
            device_id=device_at(e, f),
            device_id_type=MESH,
        )

    count = lambda flag: flag.astype(I32)
    expected = 8 - 3 * count(early) - 3 * count(late) - 2 * count(late_odd) - 4 * count(below)
    pl.semaphore_wait(barrier, expected)

    link(0, 1).start()

    @pl.when(jnp.logical_not(below))
    def _():
        link(-1, 1).start()
        link(1, 1).start()

    @pl.when(jnp.logical_not(early | late))
    def _():
        link(0, -1).start()

    @pl.when(jnp.logical_not(early | late | below))
    def _():
        link(-1, -1).start()
        link(1, -1).start()

    @pl.when(jnp.logical_not(late_odd))
    def _():
        link(-1, 0).start()
        link(1, 0).start()

    row4 = which & 3
    upper = which < 4
    own8 = jnp.concatenate([own[0:4], own[0:4]], axis=0)
    one = jnp.where(row4 == 3, 1.0, 0.0)
    zeros = jnp.zeros((2 * TYPE_PAD, GROUP), F32)
    for p in range(2):
        x = own8 + jnp.where(row4 == 2, (layer.astype(F32) - (2 * p + 0.5)) * GRID, 0.0)
        x = jnp.where(row4 == 3, 0.0, x)
        own_z[p] = x
        norm = jnp.sum(x[0:4] * x[0:4], axis=0, keepdims=True) + SOFT_CORE
        h, m, l = split3(x)
        nh, nm, nl = split3(norm)
        sides = [
            -2.0 * h + one,
            -2.0 * jnp.where(upper, m, h) + jnp.where(upper, 0.0, one),
            -2.0 * jnp.where(upper, l, m),
            jnp.where(which == 0, nh, jnp.where(which == 1, nm, jnp.where(which == 2, nl, 0.0))),
            zeros,
        ]
        rhs_w[p] = jnp.concatenate(sides, axis=0).astype(BF16)

    kinds = (iota((TYPE_PAD, GROUP), 0).astype(F32) == own[3:4]).astype(F32)
    blank = jnp.zeros((32, GROUP), F32)
    for source, target, factor in ((c6_ref, rhs_6, 6.0), (c12_ref, rhs_12, 12.0)):
        tab[...] = jnp.zeros_like(tab)
        tab[0:NTYPE, 0:NTYPE] = source[...] * factor
        coef = jnp.dot(tab[:, 0:TYPE_PAD], kinds, precision=HIGH, preferred_element_type=F32)
        first_part = coef.astype(BF16).astype(F32)
        target[...] = jnp.concatenate([blank, first_part, coef - first_part], axis=0).astype(BF16)
    wanted = jnp.broadcast_to(slot_ref[...].astype(F32), (8, GROUP)).T[:, 0:1]
    unperm[...] = (iota((GROUP, GROUP), 1).astype(F32) == wanted).astype(F32).astype(BF16)
    expand[...] = (iota((16, GROUP), 0) == iota((16, GROUP), 1) // BLOCK).astype(F32).astype(BF16)
    acc[...] = jnp.zeros_like(acc)

    inv_cut = 1.0 / (CUT_X)
    cut4 = inv_cut**4
    cut7 = inv_cut**7

    ahead = (1 - 2 * (v % 2)) * (1 - 2 * count(below))

    def wait(slot, width):
        pltpu.make_async_remote_copy(
            src_ref=rec.at[4, :, pl.ds(0, width)],
            dst_ref=rec.at[slot, :, pl.ds(0, width)],
            send_sem=send_sem.at[slot], recv_sem=recv_sem.at[slot],
            device_id=device_at(1, 0), device_id_type=MESH,
        ).wait_recv()

    def features(slot, at, scale):
        e, f = slot % 3 - 1, slot // 3 - 1
        tab_u = rec[3 + e + 1, :, GROUP : GROUP + BLOCK]
        tab_v = rec[(f + 1) * 3 + 1, :, GROUP + BLOCK : LINK]
        shift_u = BLOCK - ((1 - e) * 16 + (1 + f) * 4)
        shift_v = BLOCK - ((1 - f) * 16 + (1 + e) * 4)
        tab_u = pltpu.roll(jnp.concatenate([tab_u, tab_u], axis=0), shift_u, 1)
        tab_v = pltpu.roll(jnp.concatenate([tab_v, tab_v], axis=0), shift_v, 1)
        seen = (tab_u + tab_v)[:, 0:16]
        weight = jnp.dot(seen.astype(BF16), expand[...], preferred_element_type=F32)
        twice = jnp.where((slot == 4) & (which == layer), 0.5, 1.0)
        weight = weight * twice * scale

        beads = rec[slot, :, 0:GROUP]
        beads = jnp.concatenate([beads, beads], axis=0)
        over_u = (u + e + N_COL) // N_COL - 1
        over_v = (v + f + N_ROW) // N_ROW - 1
        shift_x = e.astype(F32) * GRID + over_u.astype(F32) * WRAP_X
        shift_y = f.astype(F32) * GRID + over_v.astype(F32) * WRAP_Y
        shift_z = ((layer & 1).astype(F32) - 0.5) * GRID
        shift = jnp.where(row4 == 0, shift_x, jnp.where(row4 == 1, shift_y, shift_z))
        x = jnp.where(row4 == 3, 0.0, beads + shift)
        norm = jnp.sum(x[0:4] * x[0:4], axis=0, keepdims=True)
        h, m, l = split3(jnp.where(row4 == 3, norm, x))
        high_mid = jnp.where(upper, h, m)
        kind_row = iota((TYPE_PAD, GROUP), 0).astype(F32)
        onehot = (kind_row == beads[3:4]).astype(F32)
        rows = jnp.concatenate(
            [high_mid, jnp.where(upper, h, l), high_mid, jnp.ones((8, GROUP), F32), onehot, onehot],
            axis=0,
        )
        for k in range(BPD):
            feat[at, k * BLOCK : (k + 1) * BLOCK, :] = rows[:, k * BLOCK : (k + 1) * BLOCK].T.astype(BF16)
        back = jnp.concatenate([high_mid, jnp.where(upper, l, 1.0)], axis=0)
        return back, weight

    def scalars(at):
        for p, m0, m1, n0, n1 in GROUPS:
            for n in range(n0, n1, CHUNK):
                side = feat[at, n : n + CHUNK, :]
                dist = jnp.dot(side, rhs_w[p, :, m0:m1], preferred_element_type=F32)
                c6 = jnp.dot(side, rhs_6[:, m0:m1], preferred_element_type=F32)
                c12 = jnp.dot(side, rhs_12[:, m0:m1], preferred_element_type=F32)
                inv = 1.0 / jnp.minimum(dist, CUT_X)
                inv2 = inv * inv
                inv3 = inv2 * inv
                inv4 = inv2 * inv2
                scalar = c12 * (inv4 * inv3 - cut7) - c6 * (inv4 - cut4)
                rounded = scalar.astype(BF16)
                high[at, n : n + CHUNK, m0:m1] = rounded
                low[at, n : n + CHUNK, m0:m1] = (scalar - rounded.astype(F32)).astype(BF16)

    def sums(at, back, weight):
        for p, m0, m1, n0, n1 in GROUPS:
            layers = range(m0 // BLOCK, m1 // BLOCK)
            pull = jnp.concatenate(
                [back[:, n0:n1] * weight[k : k + 1, n0:n1] for k in layers], axis=0
            ).astype(BF16)
            got = jnp.dot(pull, high[at, n0:n1, m0:m1], preferred_element_type=F32) + jnp.dot(
                pull, low[at, n0:n1, m0:m1], preferred_element_type=F32
            )
            for n, k in enumerate(layers):
                lanes = slice(k * BLOCK, (k + 1) * BLOCK)
                acc[p, :, lanes] += got[16 * n : 16 * n + 16, n * BLOCK : (n + 1) * BLOCK]

    def two_columns(t, carry):
        is_u = (t == 1).astype(I32)
        is_far = (t == 2).astype(I32)
        is_side = (t == 3).astype(I32)
        is_near = (t == 4).astype(I32)
        e = is_u + is_far + is_near
        f = is_far * ahead - is_near * ahead
        one_slot = (f + is_side * ahead + 1) * 3 + 1 - e
        two_slot = (f - is_side * ahead + 1) * 3 + 1 + e

        @pl.when(is_u == 1)
        def _():
            wait(one_slot, LINK)
            wait(two_slot, LINK)

            @pl.when(late_odd)
            def _():
                link(-1, 0).start()
                link(1, 0).start()

            @pl.when(below)
            def _():
                link(-1, 1).start()
                link(1, 1).start()

            @pl.when(late)
            def _():
                wait(1, LINK)
                for e in (-1, 0, 1):
                    link(e, -1).start()

        @pl.when((is_far == 1) & jnp.logical_not(late))
        def _():
            wait((ahead + 1) * 3 + 1, LINK)

        @pl.when(is_side == 1)
        def _():
            wait((1 - ahead) * 3 + 1, LINK)

            @pl.when(early)
            def _():
                link(0, -1).start()

        @pl.when(is_far + is_near == 1)
        def _():
            wait(one_slot, GROUP)
            wait(two_slot, GROUP)

        @pl.when(((is_near == 1) & early) | ((is_far == 1) & below))
        def _():
            link(-1, -1).start()
            link(1, -1).start()

        scale = jnp.minimum(t, 1).astype(F32)
        first_side = features(one_slot, 0, 1.0)
        second_side = features(two_slot, 1, scale)
        scalars(0)
        scalars(1)
        sums(0, *first_side)
        sums(1, *second_side)
        return carry

    lax.fori_loop(0, 5, two_columns, 0)

    force = jnp.zeros((8, GROUP), F32)
    for p in range(2):
        got = acc[p]
        pulled = got[0:8] + pltpu.roll(got[0:8], 4, 0) + got[8:16]
        force += own_z[p] * got[12:13] - pulled
    force = force * KICK_FACTOR
    parts = jnp.concatenate(split3(force), axis=0).astype(BF16)
    stored = jnp.dot(parts, unperm[...], preferred_element_type=F32)
    out_ref[...] = (stored[0:8] + stored[8:16] + stored[16:24])[0:3]

    for e, f in around:
        link(e, f).wait_send()


def body(positions, velocities, bead_types, slot_bead, tile_pairs, tile_count, c6_table, c12_table):
    vmem = pl.BlockSpec(memory_space=pltpu.VMEM)
    hbm = pl.BlockSpec(memory_space=pltpu.HBM)
    kick = pl.pallas_call(
        kernel,
        out_shape=pltpu.VMEM((3, GROUP), F32),
        in_specs=[hbm] * 7,
        out_specs=vmem,
        scratch_shapes=[
            pltpu.VMEM((3, GROUP), F32),
            pltpu.VMEM((1, GROUP), I32),
            pltpu.VMEM((1, GROUP), I32),
            pltpu.VMEM((2, 72), I32),
            pltpu.SMEM((1,), I32),
            pltpu.VMEM((NTYPE, NTYPE), F32),
            pltpu.VMEM((NTYPE, NTYPE), F32),
            pltpu.VMEM((9, 4, LINK), F32),
            pltpu.VMEM((GROUP, GROUP), BF16),
            pltpu.VMEM((GROUP, GROUP), BF16),
            pltpu.VMEM((8, GROUP), F32),
            pltpu.VMEM((8, BLOCK), I32),
            pltpu.VMEM((TYPE_PAD, BLOCK), F32),
            pltpu.VMEM((2, FEATURES, GROUP), BF16),
            pltpu.VMEM((FEATURES, GROUP), BF16),
            pltpu.VMEM((FEATURES, GROUP), BF16),
            pltpu.VMEM((2, 8, GROUP), F32),
            pltpu.VMEM((16, GROUP), BF16),
            pltpu.VMEM((2, GROUP, FEATURES), BF16),
            pltpu.VMEM((2, GROUP, GROUP), BF16),
            pltpu.VMEM((2, GROUP, GROUP), BF16),
            pltpu.VMEM((2, 16, GROUP), F32),
            pltpu.SemaphoreType.DMA((7,)),
            pltpu.SemaphoreType.DMA((9,)),
            pltpu.SemaphoreType.DMA((9,)),
        ],
        compiler_params=pltpu.CompilerParams(
            collective_id=0, has_side_effects=True, vmem_limit_bytes=60 * 2**20
        ),
        name="column_forces",
    )(
        positions,
        bead_types.reshape(1, GROUP),
        slot_bead.reshape(1, GROUP),
        tile_pairs,
        tile_count,
        c6_table,
        c12_table,
    )
    return velocities + kick


def solution(mesh):
    return jax.shard_map(
        body,
        mesh=mesh,
        in_specs=(
            P(None, ("row", "col")),
            P(None, ("row", "col")),
            P(("row", "col")),
            P(("row", "col")),
            P(None, ("row", "col")),
            P(("row", "col")),
            P(),
            P(),
        ),
        out_specs=P(None, ("row", "col")),
        check_vma=False,
    )
```

```python
import functools

import jax
import jax.numpy as jnp
import numpy as np
from jax import lax
from jax.experimental import pallas as pl
from jax.experimental.pallas import tpu as pltpu
from jax.sharding import PartitionSpec as P

F32 = jnp.float32
BF16 = jnp.bfloat16
I32 = jnp.int32
MESH = pl.DeviceIdType.MESH
HIGH = lax.Precision.HIGHEST

BLOCK = 128
BPD = 4
GROUP = BPD * BLOCK
N_ROW = 32
N_COL = 16
NTYPE = 18
TYPE_PAD = 24
SOFT_CORE = 0.25
CUT_SQ = 1.2 * 1.2
CELL_SIDE = 2.47
KICK_FACTOR = 0.02 / 72.0

GRID = 2.46875
WRAP_X = float(np.float32(N_COL * CELL_SIDE) - np.float32(N_COL * GRID))
WRAP_Y = float(np.float32(N_ROW * CELL_SIDE) - np.float32(N_ROW * GRID))

CUT_X = float(np.float32(CUT_SQ + SOFT_CORE))
FEATURES = 32 + 2 * TYPE_PAD
LINK = GROUP + BLOCK
TABLE_V = 64
GROUPS = (
    (0, 0, 256, 0, 256),
    (0, 256, 384, 128, 256),
    (1, 128, 256, 256, 384),
    (1, 256, 512, 256, 512),
)
CHUNK = 128
NT = (((1,), (1,)), ((), ()))


def iota(shape, dim):
    return lax.broadcasted_iota(I32, shape, dim)


def split3(x):
    high = x.astype(BF16).astype(F32)
    rest = x - high
    mid = rest.astype(BF16).astype(F32)
    return high, mid, rest - mid


def kernel(
    pos_hbm, typ_hbm, slot_hbm, pair_hbm, count_hbm, c6_hbm, c12_hbm, out_ref,
    pos_ref, typ_ref, slot_ref, pair_ref, count_ref, c6_ref, c12_ref,
    rec, perm, unperm, stage, pairs, tab, rhs_w, rhs_6, rhs_12, own_z, expand, feat, high, low, acc,
    load_sem, send_sem, recv_sem,
):
    loads = [
        pltpu.make_async_copy(source, target, load_sem.at[n])
        for n, (source, target) in enumerate((
            (slot_hbm, slot_ref), (pos_hbm, pos_ref), (typ_hbm, typ_ref), (pair_hbm, pair_ref),
            (count_hbm, count_ref), (c6_hbm, c6_ref), (c12_hbm, c12_ref),
        ))
    ]
    for load in loads[:5]:
        load.start()

    row, col = lax.axis_index("row"), lax.axis_index("col")
    u = 2 * (col % 8) + col // 8
    v = 2 * (row % 16) + row // 16

    def device_at(e, f):
        to_u = (u + e + N_COL) % N_COL
        to_v = (v + f + N_ROW) % N_ROW
        return (to_v // 2 + to_v % 2 * 16, to_u // 2 + to_u % 2 * 8)

    def slot_of(e, f):
        return (f + 1) * 3 + e + 1

    early = v % 16 == 0
    late = v % 16 == 15
    below = v % 16 == 14
    lower = v % 16 == 13
    last = v == N_ROW - 1
    before_last = v == N_ROW - 2
    even = u % 2 == 0
    half_heard = late & even & jnp.logical_not(last | (u & 13 == 8))
    barrier = pltpu.get_barrier_semaphore()

    def greet(e, f):
        pl.semaphore_signal(barrier, inc=1, device_id=device_at(e, f), device_id_type=MESH)

    greet(0, -1)

    @pl.when(jnp.logical_not(late))
    def _():
        greet(-1, -1)
        greet(1, -1)

    @pl.when(jnp.logical_not(late | before_last))
    def _():
        greet(0, 1)

    for e in (-1, 1):
        to_half_heard = below & jnp.logical_not(even | ((u + e) & 13 == 8))

        @pl.when(jnp.logical_not(late | before_last | lower | to_half_heard))
        def _():
            greet(e, 1)

    @pl.when(jnp.logical_not(late))
    def _():
        greet(-1, 0)
        greet(1, 0)

    for load in loads[5:]:
        load.start()
    for load in loads[:5]:
        load.wait()

    perm[...] = (iota((GROUP, GROUP), 0) == slot_ref[...]).astype(F32).astype(BF16)
    stage[...] = jnp.zeros_like(stage)
    stage[0:3, :] = pos_ref[...]
    stage[3:4, :] = typ_ref[...].astype(F32)
    which = iota((8, GROUP), 0)
    lane = iota((8, GROUP), 1)
    layer = lane // BLOCK
    half = GRID * 0.5
    origin = jnp.where(which == 0, u.astype(F32) * GRID + half, 0.0)
    origin = jnp.where(which == 1, v.astype(F32) * GRID + half, origin)
    parts = jnp.concatenate(split3(stage[...] - origin), axis=0).astype(BF16)
    moved = jnp.dot(parts, perm[...], preferred_element_type=F32)
    own = moved[0:8] + moved[8:16] + moved[16:24]
    own = own - jnp.where(which == 2, layer.astype(F32) * GRID + half, 0.0)
    rec[4, :, 0:GROUP] = own[0:4]

    pairs[...] = jnp.zeros_like(pairs)
    pairs[0:2, 0:72] = pair_ref[...]
    code = pairs[...]
    first, second = code[0:1], code[1:2]
    at_a = 2 * ((first >> 2) & 7) + (first >> 5)
    at_b = 2 * ((second >> 2) & 15) + (second >> 6)
    du = (at_a - u + 1) & (N_COL - 1)
    dv = (at_b - v + 1) & (N_ROW - 1)
    ka, kb = first & 3, second & 3
    live = iota((1, BLOCK), 1) < count_ref[0]
    eight = iota((8, BLOCK), 0)
    full = iota((BLOCK, BLOCK), 0)

    def table(layer_at, at):
        left = jnp.where((eight == layer_at) & live, 1.0, 0.0).astype(BF16)
        right = jnp.where(full == at, 1.0, 0.0).astype(BF16)
        return lax.dot_general(left, right, NT, preferred_element_type=F32)

    tables = table(ka, du * 16 + dv * 4 + kb) + table(kb, TABLE_V + dv * 16 + du * 4 + ka)
    rec[4, :, GROUP:LINK] = tables[0:4]

    def link(e, f, width=None):
        width = width or (GROUP if e and f else LINK)
        return pltpu.make_async_remote_copy(
            src_ref=rec.at[4, :, pl.ds(0, width)],
            dst_ref=rec.at[slot_of(-e, -f), :, pl.ds(0, width)],
            send_sem=send_sem.at[slot_of(e, f)],
            recv_sem=recv_sem.at[slot_of(-e, -f)],
            device_id=device_at(e, f),
            device_id_type=MESH,
        )

    def forward(e, f, width):
        return pltpu.make_async_remote_copy(
            src_ref=rec.at[slot_of(e, f), :, pl.ds(0, width)],
            dst_ref=rec.at[slot_of(e, f + 1), :, pl.ds(0, width)],
            send_sem=send_sem.at[slot_of(e, -1) if f == 0 else 9 + (e + 1) // 2],
            recv_sem=recv_sem.at[slot_of(e, f + 1)],
            device_id=device_at(0, -1),
            device_id_type=MESH,
        )

    count = lambda flag: flag.astype(I32)
    expected = 8 - 3 * count(early) - 2 * count(late) - 3 * count(last) - 4 * count(below) - 2 * count(half_heard)
    pl.semaphore_wait(barrier, expected)

    @pl.when(late)
    def _():
        link(-1, 1, LINK).start()
        link(1, 1, LINK).start()

    link(0, 1).start()

    @pl.when(jnp.logical_not(late | below))
    def _():
        link(-1, 1).start()
        link(1, 1).start()

    @pl.when(jnp.logical_not(early | last))
    def _():
        link(0, -1).start()

    @pl.when(jnp.logical_not(early | last | half_heard | below))
    def _():
        link(-1, -1).start()
        link(1, -1).start()

    @pl.when(jnp.logical_not(late))
    def _():
        link(-1, 0).start()
        link(1, 0).start()

    row4 = which & 3
    upper = which < 4
    own8 = jnp.concatenate([own[0:4], own[0:4]], axis=0)
    one = jnp.where(row4 == 3, 1.0, 0.0)
    zeros = jnp.zeros((2 * TYPE_PAD, GROUP), F32)
    for p in range(2):
        x = own8 + jnp.where(row4 == 2, (layer.astype(F32) - (2 * p + 0.5)) * GRID, 0.0)
        x = jnp.where(row4 == 3, 0.0, x)
        own_z[p] = x
        norm = jnp.sum(x[0:4] * x[0:4], axis=0, keepdims=True) + SOFT_CORE
        h, m, l = split3(x)
        nh, nm, nl = split3(norm)
        sides = [
            -2.0 * h + one,
            -2.0 * jnp.where(upper, m, h) + jnp.where(upper, 0.0, one),
            -2.0 * jnp.where(upper, l, m),
            jnp.where(which == 0, nh, jnp.where(which == 1, nm, jnp.where(which == 2, nl, 0.0))),
            zeros,
        ]
        rhs_w[p] = jnp.concatenate(sides, axis=0).astype(BF16)

    for load in loads[5:]:
        load.wait()
    kinds = (iota((TYPE_PAD, GROUP), 0).astype(F32) == own[3:4]).astype(F32)
    blank = jnp.zeros((32, GROUP), F32)
    for source, target, factor in ((c6_ref, rhs_6, 6.0), (c12_ref, rhs_12, 12.0)):
        tab[...] = jnp.zeros_like(tab)
        tab[0:NTYPE, 0:NTYPE] = source[...] * factor
        coef = jnp.dot(tab[:, 0:TYPE_PAD], kinds, precision=HIGH, preferred_element_type=F32)
        first_part = coef.astype(BF16).astype(F32)
        target[...] = jnp.concatenate([blank, first_part, coef - first_part], axis=0).astype(BF16)
    wanted = jnp.broadcast_to(slot_ref[...].astype(F32), (8, GROUP)).T[:, 0:1]
    unperm[...] = (iota((GROUP, GROUP), 1).astype(F32) == wanted).astype(F32).astype(BF16)
    expand[...] = (iota((16, GROUP), 0) == iota((16, GROUP), 1) // BLOCK).astype(F32).astype(BF16)
    acc[...] = jnp.zeros_like(acc)

    inv_cut = 1.0 / (CUT_X)
    cut4 = inv_cut**4
    cut7 = inv_cut**7

    ahead = (1 - 2 * (v % 2)) * (1 - 2 * count(before_last))

    def wait(slot, width):
        pltpu.make_async_remote_copy(
            src_ref=rec.at[4, :, pl.ds(0, width)],
            dst_ref=rec.at[slot, :, pl.ds(0, width)],
            send_sem=send_sem.at[slot], recv_sem=recv_sem.at[slot],
            device_id=device_at(1, 0), device_id_type=MESH,
        ).wait_recv()

    def features(slot, at, scale):
        e, f = slot % 3 - 1, slot // 3 - 1
        tab_u = rec[3 + e + 1, :, GROUP:LINK]
        tab_v = rec[(f + 1) * 3 + 1, :, GROUP:LINK]
        shift_u = BLOCK - ((1 - e) * 16 + (1 + f) * 4)
        shift_v = BLOCK - (TABLE_V + (1 - f) * 16 + (1 + e) * 4)
        tab_u = pltpu.roll(jnp.concatenate([tab_u, tab_u], axis=0), shift_u, 1)
        tab_v = pltpu.roll(jnp.concatenate([tab_v, tab_v], axis=0), shift_v, 1)
        seen = (tab_u + tab_v)[:, 0:16]
        weight = jnp.dot(seen.astype(BF16), expand[...], preferred_element_type=F32)
        twice = jnp.where((slot == 4) & (which == layer), 0.5, 1.0)
        weight = weight * twice * scale

        beads = rec[slot, :, 0:GROUP]
        beads = jnp.concatenate([beads, beads], axis=0)
        over_u = (u + e + N_COL) // N_COL - 1
        over_v = (v + f + N_ROW) // N_ROW - 1
        shift_x = e.astype(F32) * GRID + over_u.astype(F32) * WRAP_X
        shift_y = f.astype(F32) * GRID + over_v.astype(F32) * WRAP_Y
        shift_z = ((layer & 1).astype(F32) - 0.5) * GRID
        shift = jnp.where(row4 == 0, shift_x, jnp.where(row4 == 1, shift_y, shift_z))
        x = jnp.where(row4 == 3, 0.0, beads + shift)
        norm = jnp.sum(x[0:4] * x[0:4], axis=0, keepdims=True)
        h, m, l = split3(jnp.where(row4 == 3, norm, x))
        high_mid = jnp.where(upper, h, m)
        kind_row = iota((TYPE_PAD, GROUP), 0).astype(F32)
        onehot = (kind_row == beads[3:4]).astype(F32)
        rows = jnp.concatenate(
            [high_mid, jnp.where(upper, h, l), high_mid, jnp.ones((8, GROUP), F32), onehot, onehot],
            axis=0,
        ).astype(BF16)
        for k in range(BPD):
            feat[at, k * BLOCK : (k + 1) * BLOCK, :] = rows[:, k * BLOCK : (k + 1) * BLOCK].T
        back = jnp.concatenate([high_mid, jnp.where(upper, l, 1.0)], axis=0)
        return back, weight

    def scalars(at):
        for p, m0, m1, n0, n1 in GROUPS:
            for n in range(n0, n1, CHUNK):
                side = feat[at, n : n + CHUNK, :]
                dist = jnp.dot(side, rhs_w[p, :, m0:m1], preferred_element_type=F32)
                c6 = jnp.dot(side, rhs_6[:, m0:m1], preferred_element_type=F32)
                c12 = jnp.dot(side, rhs_12[:, m0:m1], preferred_element_type=F32)
                inv = 1.0 / jnp.minimum(dist, CUT_X)
                inv2 = inv * inv
                inv3 = inv2 * inv
                inv4 = inv2 * inv2
                scalar = c12 * (inv4 * inv3 - cut7) - c6 * (inv4 - cut4)
                rounded = scalar.astype(BF16)
                high[at, n : n + CHUNK, m0:m1] = rounded
                low[at, n : n + CHUNK, m0:m1] = (scalar - rounded.astype(F32)).astype(BF16)

    def sums(at, back, weight):
        for p, m0, m1, n0, n1 in GROUPS:
            layers = range(m0 // BLOCK, m1 // BLOCK)
            pull = jnp.concatenate(
                [back[:, n0:n1] * weight[k : k + 1, n0:n1] for k in layers], axis=0
            ).astype(BF16)
            got = jnp.dot(pull, high[at, n0:n1, m0:m1], preferred_element_type=F32) + jnp.dot(
                pull, low[at, n0:n1, m0:m1], preferred_element_type=F32
            )
            for n, k in enumerate(layers):
                lanes = slice(k * BLOCK, (k + 1) * BLOCK)
                acc[p, :, lanes] += got[16 * n : 16 * n + 16, n * BLOCK : (n + 1) * BLOCK]

    def two_columns(t, carry):
        is_u = (t == 1).astype(I32)
        side_at = 3 - count(v == 0)
        is_far = (t == 5 - side_at).astype(I32)
        is_side = (t == side_at).astype(I32)
        is_near = (t == 4).astype(I32)
        e = is_u + is_far + is_near
        f = is_far * ahead - is_near * ahead
        one_slot = (f + is_side * ahead + 1) * 3 + 1 - e
        two_slot = (f - is_side * ahead + 1) * 3 + 1 + e

        @pl.when((is_u == 1) & (last | half_heard))
        def _():
            wait(1, LINK)
            link(-1, -1).start()
            link(1, -1).start()

            @pl.when(last)
            def _():
                link(0, -1).start()

        @pl.when(is_u == 1)
        def _():
            wait(one_slot, LINK)
            wait(two_slot, LINK)

            @pl.when(below)
            def _():
                for f in (-1, 1):
                    link(-1, f).start()
                    link(1, f).start()

        @pl.when((t == 2) & jnp.logical_not(last | half_heard))
        def _():
            wait((ahead + 1) * 3 + 1, LINK)

        @pl.when(is_side == 1)
        def _():
            wait((1 - ahead) * 3 + 1, LINK)

            @pl.when(early)
            def _():
                link(0, -1).start()
                forward(-1, 0, GROUP).start()
                forward(1, 0, GROUP).start()

        from_late = (is_near == 1) & early

        @pl.when((is_far + is_near == 1) & jnp.logical_not(from_late))
        def _():
            wait(one_slot, GROUP)
            wait(two_slot, GROUP)

        @pl.when(from_late)
        def _():
            for side in (-1, 1):
                wait(slot_of(side, -1), LINK)
                forward(side, -1, LINK).start()

        scale = jnp.minimum(t, 1).astype(F32)
        first_side = features(one_slot, 0, 1.0)
        second_side = features(two_slot, 1, scale)
        scalars(0)
        sums(0, *first_side)
        scalars(1)
        sums(1, *second_side)
        return carry

    lax.fori_loop(0, 5, two_columns, 0)

    force = jnp.zeros((8, GROUP), F32)
    for p in range(2):
        got = acc[p]
        pulled = got[0:8] + pltpu.roll(got[0:8], 4, 0) + got[8:16]
        force += own_z[p] * got[12:13] - pulled
    force = force * KICK_FACTOR
    parts = jnp.concatenate(split3(force), axis=0).astype(BF16)
    stored = jnp.dot(parts, unperm[...], preferred_element_type=F32)
    out_ref[...] = (stored[0:8] + stored[8:16] + stored[16:24])[0:3]

    for e in (-1, 0, 1):
        link(e, -1).wait_send()
    link(0, 1).wait_send()

    @pl.when(late)
    def _():
        link(-1, 1, LINK).wait_send()
        link(1, 1, LINK).wait_send()

    @pl.when(jnp.logical_not(late))
    def _():
        for e in (-1, 1):
            link(e, 1).wait_send()
            link(e, 0).wait_send()

    @pl.when(early)
    def _():
        forward(-1, -1, LINK).wait_send()
        forward(1, -1, LINK).wait_send()


def body(positions, velocities, bead_types, slot_bead, tile_pairs, tile_count, c6_table, c12_table):
    vmem = pl.BlockSpec(memory_space=pltpu.VMEM)
    hbm = pl.BlockSpec(memory_space=pltpu.HBM)
    kick = pl.pallas_call(
        kernel,
        out_shape=pltpu.VMEM((3, GROUP), F32),
        in_specs=[hbm] * 7,
        out_specs=vmem,
        scratch_shapes=[
            pltpu.VMEM((3, GROUP), F32),
            pltpu.VMEM((1, GROUP), I32),
            pltpu.VMEM((1, GROUP), I32),
            pltpu.VMEM((2, 72), I32),
            pltpu.SMEM((1,), I32),
            pltpu.VMEM((NTYPE, NTYPE), F32),
            pltpu.VMEM((NTYPE, NTYPE), F32),
            pltpu.VMEM((9, 4, LINK), F32),
            pltpu.VMEM((GROUP, GROUP), BF16),
            pltpu.VMEM((GROUP, GROUP), BF16),
            pltpu.VMEM((8, GROUP), F32),
            pltpu.VMEM((8, BLOCK), I32),
            pltpu.VMEM((TYPE_PAD, BLOCK), F32),
            pltpu.VMEM((2, FEATURES, GROUP), BF16),
            pltpu.VMEM((FEATURES, GROUP), BF16),
            pltpu.VMEM((FEATURES, GROUP), BF16),
            pltpu.VMEM((2, 8, GROUP), F32),
            pltpu.VMEM((16, GROUP), BF16),
            pltpu.VMEM((2, GROUP, FEATURES), BF16),
            pltpu.VMEM((2, GROUP, GROUP), BF16),
            pltpu.VMEM((2, GROUP, GROUP), BF16),
            pltpu.VMEM((2, 16, GROUP), F32),
            pltpu.SemaphoreType.DMA((7,)),
            pltpu.SemaphoreType.DMA((11,)),
            pltpu.SemaphoreType.DMA((9,)),
        ],
        compiler_params=pltpu.CompilerParams(
            collective_id=0, has_side_effects=True, vmem_limit_bytes=60 * 2**20
        ),
        name="column_forces",
    )(
        positions,
        bead_types.reshape(1, GROUP),
        slot_bead.reshape(1, GROUP),
        tile_pairs,
        tile_count,
        c6_table,
        c12_table,
    )
    return velocities + kick


def solution(mesh):
    return jax.shard_map(
        body,
        mesh=mesh,
        in_specs=(
            P(None, ("row", "col")),
            P(None, ("row", "col")),
            P(("row", "col")),
            P(("row", "col")),
            P(None, ("row", "col")),
            P(("row", "col")),
            P(),
            P(),
        ),
        out_specs=P(None, ("row", "col")),
        check_vma=False,
    )
```

```python
import functools

import jax
import jax.numpy as jnp
import numpy as np
from jax import lax
from jax.experimental import pallas as pl
from jax.experimental.pallas import tpu as pltpu
from jax.sharding import PartitionSpec as P

F32 = jnp.float32
BF16 = jnp.bfloat16
I32 = jnp.int32
MESH = pl.DeviceIdType.MESH
HIGH = lax.Precision.HIGHEST

BLOCK = 128
BPD = 4
GROUP = BPD * BLOCK
N_ROW = 32
N_COL = 16
NTYPE = 18
TYPE_PAD = 24
SOFT_CORE = 0.25
CUT_SQ = 1.2 * 1.2
CELL_SIDE = 2.47
KICK_FACTOR = 0.02 / 72.0

GRID = 2.46875
WRAP_X = float(np.float32(N_COL * CELL_SIDE) - np.float32(N_COL * GRID))
WRAP_Y = float(np.float32(N_ROW * CELL_SIDE) - np.float32(N_ROW * GRID))

CUT_X = float(np.float32(CUT_SQ + SOFT_CORE))
FEATURES = 32 + 2 * TYPE_PAD
LINK = GROUP + BLOCK
TABLE_V = 64
GROUPS = (
    (0, 0, 256, 0, 256),
    (0, 256, 384, 128, 256),
    (1, 128, 256, 256, 384),
    (1, 256, 512, 256, 512),
)
CHUNK = 128
NT = (((1,), (1,)), ((), ()))


def iota(shape, dim):
    return lax.broadcasted_iota(I32, shape, dim)


def split3(x):
    high = x.astype(BF16).astype(F32)
    rest = x - high
    mid = rest.astype(BF16).astype(F32)
    return high, mid, rest - mid


def kernel(
    pos_hbm, typ_hbm, slot_hbm, pair_hbm, count_hbm, c6_hbm, c12_hbm, out_ref,
    pos_ref, typ_ref, slot_ref, pair_ref, count_ref, c6_ref, c12_ref,
    rec, perm, unperm, stage, pairs, tab, rhs_w, rhs_6, rhs_12, own_z, expand, feat, high, low, acc,
    load_sem, send_sem, recv_sem,
):
    loads = [
        pltpu.make_async_copy(source, target, load_sem.at[n])
        for n, (source, target) in enumerate((
            (slot_hbm, slot_ref), (pos_hbm, pos_ref), (typ_hbm, typ_ref), (pair_hbm, pair_ref),
            (count_hbm, count_ref), (c6_hbm, c6_ref), (c12_hbm, c12_ref),
        ))
    ]
    for load in loads[:5]:
        load.start()

    row, col = lax.axis_index("row"), lax.axis_index("col")
    u = 2 * (col % 8) + col // 8
    v = 2 * (row % 16) + row // 16

    def device_at(e, f):
        to_u = (u + e + N_COL) % N_COL
        to_v = (v + f + N_ROW) % N_ROW
        return (to_v // 2 + to_v % 2 * 16, to_u // 2 + to_u % 2 * 8)

    def slot_of(e, f):
        return (f + 1) * 3 + e + 1

    early = v % 16 == 0
    late = v % 16 == 15
    below = v % 16 == 14
    lower = v % 16 == 13
    last = v == N_ROW - 1
    before_last = v == N_ROW - 2
    even = u % 2 == 0
    half_heard = late & even & jnp.logical_not(last | (u & 13 == 8))
    barrier = pltpu.get_barrier_semaphore()

    def greet(e, f):
        pl.semaphore_signal(barrier, inc=1, device_id=device_at(e, f), device_id_type=MESH)

    greet(0, -1)

    @pl.when(jnp.logical_not(late))
    def _():
        greet(-1, -1)
        greet(1, -1)

    @pl.when(jnp.logical_not(late | before_last))
    def _():
        greet(0, 1)

    for e in (-1, 1):
        to_half_heard = below & jnp.logical_not(even | ((u + e) & 13 == 8))

        @pl.when(jnp.logical_not(late | before_last | lower | to_half_heard))
        def _():
            greet(e, 1)

    @pl.when(jnp.logical_not(late))
    def _():
        greet(-1, 0)
        greet(1, 0)

    for load in loads[5:]:
        load.start()
    loads[0].wait()
    perm[...] = (iota((GROUP, GROUP), 0) == slot_ref[...]).astype(F32).astype(BF16)
    for load in loads[1:5]:
        load.wait()
    stage[...] = jnp.zeros_like(stage)
    stage[0:3, :] = pos_ref[...]
    stage[3:4, :] = typ_ref[...].astype(F32)
    which = iota((8, GROUP), 0)
    lane = iota((8, GROUP), 1)
    layer = lane // BLOCK
    half = GRID * 0.5
    origin = jnp.where(which == 0, u.astype(F32) * GRID + half, 0.0)
    origin = jnp.where(which == 1, v.astype(F32) * GRID + half, origin)
    parts = jnp.concatenate(split3(stage[...] - origin), axis=0).astype(BF16)
    moved = jnp.dot(parts, perm[...], preferred_element_type=F32)
    own = moved[0:8] + moved[8:16] + moved[16:24]
    own = own - jnp.where(which == 2, layer.astype(F32) * GRID + half, 0.0)
    rec[4, :, 0:GROUP] = own[0:4]

    pairs[...] = jnp.zeros_like(pairs)
    pairs[0:2, 0:72] = pair_ref[...]
    code = pairs[...]
    first, second = code[0:1], code[1:2]
    at_a = 2 * ((first >> 2) & 7) + (first >> 5)
    at_b = 2 * ((second >> 2) & 15) + (second >> 6)
    du = (at_a - u + 1) & (N_COL - 1)
    dv = (at_b - v + 1) & (N_ROW - 1)
    ka, kb = first & 3, second & 3
    live = iota((1, BLOCK), 1) < count_ref[0]
    eight = iota((8, BLOCK), 0)
    full = iota((BLOCK, BLOCK), 0)

    left = jnp.concatenate([eight == ka, eight == kb], axis=1)
    left = jnp.where(left & jnp.concatenate([live, live], axis=1), 1.0, 0.0).astype(BF16)
    at_u = du * 16 + dv * 4 + kb
    at_v = TABLE_V + dv * 16 + du * 4 + ka
    right = jnp.concatenate([full == at_u, full == at_v], axis=1)
    right = jnp.where(right, 1.0, 0.0).astype(BF16)
    rec[4, :, GROUP:LINK] = lax.dot_general(left, right, NT, preferred_element_type=F32)[0:4]

    def link(e, f, width=None):
        width = width or (GROUP if e and f else LINK)
        return pltpu.make_async_remote_copy(
            src_ref=rec.at[4, :, pl.ds(0, width)],
            dst_ref=rec.at[slot_of(-e, -f), :, pl.ds(0, width)],
            send_sem=send_sem.at[slot_of(e, f)],
            recv_sem=recv_sem.at[slot_of(-e, -f)],
            device_id=device_at(e, f),
            device_id_type=MESH,
        )

    def forward(e, f, width):
        return pltpu.make_async_remote_copy(
            src_ref=rec.at[slot_of(e, f), :, pl.ds(0, width)],
            dst_ref=rec.at[slot_of(e, f + 1), :, pl.ds(0, width)],
            send_sem=send_sem.at[slot_of(e, -1) if f == 0 else 9 + (e + 1) // 2],
            recv_sem=recv_sem.at[slot_of(e, f + 1)],
            device_id=device_at(0, -1),
            device_id_type=MESH,
        )

    count = lambda flag: flag.astype(I32)
    expected = 8 - 3 * count(early) - 2 * count(late) - 3 * count(last) - 4 * count(below) - 2 * count(half_heard)
    pl.semaphore_wait(barrier, expected)

    @pl.when(late)
    def _():
        link(-1, 1, LINK).start()
        link(1, 1, LINK).start()

    link(0, 1).start()

    @pl.when(jnp.logical_not(late | below))
    def _():
        link(-1, 1).start()
        link(1, 1).start()

    @pl.when(jnp.logical_not(early | last))
    def _():
        link(0, -1).start()

    @pl.when(jnp.logical_not(early | last | half_heard | below))
    def _():
        link(-1, -1).start()
        link(1, -1).start()

    @pl.when(jnp.logical_not(late))
    def _():
        link(-1, 0).start()
        link(1, 0).start()

    row4 = which & 3
    upper = which < 4
    own8 = jnp.concatenate([own[0:4], own[0:4]], axis=0)
    one = jnp.where(row4 == 3, 1.0, 0.0)
    zeros = jnp.zeros((2 * TYPE_PAD, GROUP), F32)
    for p in range(2):
        x = own8 + jnp.where(row4 == 2, (layer.astype(F32) - (2 * p + 0.5)) * GRID, 0.0)
        x = jnp.where(row4 == 3, 0.0, x)
        own_z[p] = x
        norm = jnp.sum(x[0:4] * x[0:4], axis=0, keepdims=True) + SOFT_CORE
        h, m, l = split3(x)
        nh, nm, nl = split3(norm)
        sides = [
            -2.0 * h + one,
            -2.0 * jnp.where(upper, m, h) + jnp.where(upper, 0.0, one),
            -2.0 * jnp.where(upper, l, m),
            jnp.where(which == 0, nh, jnp.where(which == 1, nm, jnp.where(which == 2, nl, 0.0))),
            zeros,
        ]
        rhs_w[p] = jnp.concatenate(sides, axis=0).astype(BF16)

    for load in loads[5:]:
        load.wait()
    kinds = (iota((TYPE_PAD, GROUP), 0).astype(F32) == own[3:4]).astype(F32)
    blank = jnp.zeros((32, GROUP), F32)
    for source, target, factor in ((c6_ref, rhs_6, 6.0), (c12_ref, rhs_12, 12.0)):
        tab[...] = jnp.zeros_like(tab)
        tab[0:NTYPE, 0:NTYPE] = source[...] * factor
        coef = jnp.dot(tab[:, 0:TYPE_PAD], kinds, precision=HIGH, preferred_element_type=F32)
        first_part = coef.astype(BF16).astype(F32)
        target[...] = jnp.concatenate([blank, first_part, coef - first_part], axis=0).astype(BF16)
    wanted = jnp.broadcast_to(slot_ref[...].astype(F32), (8, GROUP)).T[:, 0:1]
    unperm[...] = (iota((GROUP, GROUP), 1).astype(F32) == wanted).astype(F32).astype(BF16)
    expand[...] = (iota((16, GROUP), 0) == iota((16, GROUP), 1) // BLOCK).astype(F32).astype(BF16)
    acc[...] = jnp.zeros_like(acc)

    inv_cut = 1.0 / (CUT_X)
    cut4 = inv_cut**4
    cut7 = inv_cut**7

    ahead = (1 - 2 * (v % 2)) * (1 - 2 * count(before_last))

    def wait(slot, width):
        pltpu.make_async_remote_copy(
            src_ref=rec.at[4, :, pl.ds(0, width)],
            dst_ref=rec.at[slot, :, pl.ds(0, width)],
            send_sem=send_sem.at[slot], recv_sem=recv_sem.at[slot],
            device_id=device_at(1, 0), device_id_type=MESH,
        ).wait_recv()

    def features(slot, at, scale):
        e, f = slot % 3 - 1, slot // 3 - 1
        tab_u = rec[3 + e + 1, :, GROUP:LINK]
        tab_v = rec[(f + 1) * 3 + 1, :, GROUP:LINK]
        shift_u = BLOCK - ((1 - e) * 16 + (1 + f) * 4)
        shift_v = BLOCK - (TABLE_V + (1 - f) * 16 + (1 + e) * 4)
        tab_u = pltpu.roll(jnp.concatenate([tab_u, tab_u], axis=0), shift_u, 1)
        tab_v = pltpu.roll(jnp.concatenate([tab_v, tab_v], axis=0), shift_v, 1)
        seen = (tab_u + tab_v)[:, 0:16]
        weight = jnp.dot(seen.astype(BF16), expand[...], preferred_element_type=F32)
        twice = jnp.where((slot == 4) & (which == layer), 0.5, 1.0)
        weight = weight * twice * scale

        beads = rec[slot, :, 0:GROUP]
        beads = jnp.concatenate([beads, beads], axis=0)
        over_u = (u + e + N_COL) // N_COL - 1
        over_v = (v + f + N_ROW) // N_ROW - 1
        shift_x = e.astype(F32) * GRID + over_u.astype(F32) * WRAP_X
        shift_y = f.astype(F32) * GRID + over_v.astype(F32) * WRAP_Y
        shift_z = ((layer & 1).astype(F32) - 0.5) * GRID
        shift = jnp.where(row4 == 0, shift_x, jnp.where(row4 == 1, shift_y, shift_z))
        x = jnp.where(row4 == 3, 0.0, beads + shift)
        norm = jnp.sum(x[0:4] * x[0:4], axis=0, keepdims=True)
        h, m, l = split3(jnp.where(row4 == 3, norm, x))
        high_mid = jnp.where(upper, h, m)
        kind_row = iota((TYPE_PAD, GROUP), 0).astype(F32)
        onehot = (kind_row == beads[3:4]).astype(F32)
        rows = jnp.concatenate(
            [high_mid, jnp.where(upper, h, l), high_mid, jnp.ones((8, GROUP), F32), onehot, onehot],
            axis=0,
        ).astype(BF16)
        for k in range(BPD):
            feat[at, k * BLOCK : (k + 1) * BLOCK, :] = rows[:, k * BLOCK : (k + 1) * BLOCK].T
        back = jnp.concatenate([high_mid, jnp.where(upper, l, 1.0)], axis=0)
        return back, weight

    def scalars(at):
        for p, m0, m1, n0, n1 in GROUPS:
            for n in range(n0, n1, CHUNK):
                side = feat[at, n : n + CHUNK, :]
                dist = jnp.dot(side, rhs_w[p, :, m0:m1], preferred_element_type=F32)
                c6 = jnp.dot(side, rhs_6[:, m0:m1], preferred_element_type=F32)
                c12 = jnp.dot(side, rhs_12[:, m0:m1], preferred_element_type=F32)
                inv = 1.0 / jnp.minimum(dist, CUT_X)
                inv2 = inv * inv
                inv3 = inv2 * inv
                inv4 = inv2 * inv2
                scalar = c12 * (inv4 * inv3 - cut7) - c6 * (inv4 - cut4)
                rounded = scalar.astype(BF16)
                high[at, n : n + CHUNK, m0:m1] = rounded
                low[at, n : n + CHUNK, m0:m1] = (scalar - rounded.astype(F32)).astype(BF16)

    def sums(at, back, weight):
        for p, m0, m1, n0, n1 in GROUPS:
            layers = range(m0 // BLOCK, m1 // BLOCK)
            pull = jnp.concatenate(
                [back[:, n0:n1] * weight[k : k + 1, n0:n1] for k in layers], axis=0
            ).astype(BF16)
            got = jnp.dot(pull, high[at, n0:n1, m0:m1], preferred_element_type=F32) + jnp.dot(
                pull, low[at, n0:n1, m0:m1], preferred_element_type=F32
            )
            for n, k in enumerate(layers):
                lanes = slice(k * BLOCK, (k + 1) * BLOCK)
                acc[p, :, lanes] += got[16 * n : 16 * n + 16, n * BLOCK : (n + 1) * BLOCK]

    def two_columns(t, carry):
        is_u = (t == 1).astype(I32)
        side_at = 3 - count(v == 0)
        is_far = (t == 5 - side_at).astype(I32)
        is_side = (t == side_at).astype(I32)
        is_near = (t == 4).astype(I32)
        e = is_u + is_far + is_near
        f = is_far * ahead - is_near * ahead
        one_slot = (f + is_side * ahead + 1) * 3 + 1 - e
        two_slot = (f - is_side * ahead + 1) * 3 + 1 + e

        @pl.when((is_u == 1) & (last | half_heard))
        def _():
            wait(1, LINK)
            link(-1, -1).start()
            link(1, -1).start()

            @pl.when(last)
            def _():
                link(0, -1).start()

        @pl.when(is_u == 1)
        def _():
            wait(one_slot, LINK)
            wait(two_slot, LINK)

            @pl.when(below)
            def _():
                for f in (-1, 1):
                    link(-1, f).start()
                    link(1, f).start()

        @pl.when((t == 2) & jnp.logical_not(last | half_heard))
        def _():
            wait((ahead + 1) * 3 + 1, LINK)

        @pl.when(is_side == 1)
        def _():
            wait((1 - ahead) * 3 + 1, LINK)

            @pl.when(early)
            def _():
                link(0, -1).start()
                forward(-1, 0, GROUP).start()
                forward(1, 0, GROUP).start()

        from_late = (is_near == 1) & early

        @pl.when((is_far + is_near == 1) & jnp.logical_not(from_late))
        def _():
            wait(one_slot, GROUP)
            wait(two_slot, GROUP)

        @pl.when(from_late)
        def _():
            for side in (-1, 1):
                wait(slot_of(side, -1), LINK)
                forward(side, -1, LINK).start()

        scale = jnp.minimum(t, 1).astype(F32)
        first_side = features(one_slot, 0, 1.0)
        second_side = features(two_slot, 1, scale)
        scalars(0)
        sums(0, *first_side)
        scalars(1)
        sums(1, *second_side)
        return carry

    lax.fori_loop(0, 5, two_columns, 0)

    force = jnp.zeros((8, GROUP), F32)
    for p in range(2):
        got = acc[p]
        pulled = got[0:8] + pltpu.roll(got[0:8], 4, 0) + got[8:16]
        force += own_z[p] * got[12:13] - pulled
    force = force * KICK_FACTOR
    coarse = force.astype(BF16).astype(F32)
    parts = jnp.concatenate([coarse, force - coarse], axis=0).astype(BF16)
    stored = jnp.dot(parts, unperm[...], preferred_element_type=F32)
    out_ref[...] = (stored[0:8] + stored[8:16])[0:3]

    for e in (-1, 0, 1):
        link(e, -1).wait_send()
    link(0, 1).wait_send()

    @pl.when(late)
    def _():
        link(-1, 1, LINK).wait_send()
        link(1, 1, LINK).wait_send()

    @pl.when(jnp.logical_not(late))
    def _():
        for e in (-1, 1):
            link(e, 1).wait_send()
            link(e, 0).wait_send()

    @pl.when(early)
    def _():
        forward(-1, -1, LINK).wait_send()
        forward(1, -1, LINK).wait_send()


def body(positions, velocities, bead_types, slot_bead, tile_pairs, tile_count, c6_table, c12_table):
    vmem = pl.BlockSpec(memory_space=pltpu.VMEM)
    hbm = pl.BlockSpec(memory_space=pltpu.HBM)
    kick = pl.pallas_call(
        kernel,
        out_shape=pltpu.VMEM((3, GROUP), F32),
        in_specs=[hbm] * 7,
        out_specs=vmem,
        scratch_shapes=[
            pltpu.VMEM((3, GROUP), F32),
            pltpu.VMEM((1, GROUP), I32),
            pltpu.VMEM((1, GROUP), I32),
            pltpu.VMEM((2, 72), I32),
            pltpu.SMEM((1,), I32),
            pltpu.VMEM((NTYPE, NTYPE), F32),
            pltpu.VMEM((NTYPE, NTYPE), F32),
            pltpu.VMEM((9, 4, LINK), F32),
            pltpu.VMEM((GROUP, GROUP), BF16),
            pltpu.VMEM((GROUP, GROUP), BF16),
            pltpu.VMEM((8, GROUP), F32),
            pltpu.VMEM((8, BLOCK), I32),
            pltpu.VMEM((TYPE_PAD, BLOCK), F32),
            pltpu.VMEM((2, FEATURES, GROUP), BF16),
            pltpu.VMEM((FEATURES, GROUP), BF16),
            pltpu.VMEM((FEATURES, GROUP), BF16),
            pltpu.VMEM((2, 8, GROUP), F32),
            pltpu.VMEM((16, GROUP), BF16),
            pltpu.VMEM((2, GROUP, FEATURES), BF16),
            pltpu.VMEM((2, GROUP, GROUP), BF16),
            pltpu.VMEM((2, GROUP, GROUP), BF16),
            pltpu.VMEM((2, 16, GROUP), F32),
            pltpu.SemaphoreType.DMA((7,)),
            pltpu.SemaphoreType.DMA((11,)),
            pltpu.SemaphoreType.DMA((9,)),
        ],
        compiler_params=pltpu.CompilerParams(
            collective_id=0, has_side_effects=True, vmem_limit_bytes=60 * 2**20
        ),
        name="column_forces",
    )(
        positions,
        bead_types.reshape(1, GROUP),
        slot_bead.reshape(1, GROUP),
        tile_pairs,
        tile_count,
        c6_table,
        c12_table,
    )
    return velocities + kick


def solution(mesh):
    return jax.shard_map(
        body,
        mesh=mesh,
        in_specs=(
            P(None, ("row", "col")),
            P(None, ("row", "col")),
            P(("row", "col")),
            P(("row", "col")),
            P(None, ("row", "col")),
            P(("row", "col")),
            P(),
            P(),
        ),
        out_specs=P(None, ("row", "col")),
        check_vma=False,
    )
```

```python
import functools

import jax
import jax.numpy as jnp
import numpy as np
from jax import lax
from jax.experimental import pallas as pl
from jax.experimental.pallas import tpu as pltpu
from jax.sharding import PartitionSpec as P

F32 = jnp.float32
BF16 = jnp.bfloat16
I32 = jnp.int32
MESH = pl.DeviceIdType.MESH
HIGH = lax.Precision.HIGHEST

BLOCK = 128
BPD = 4
GROUP = BPD * BLOCK
N_ROW = 32
N_COL = 16
NTYPE = 18
TYPE_PAD = 24
SOFT_CORE = 0.25
CUT_SQ = 1.2 * 1.2
CELL_SIDE = 2.47
KICK_FACTOR = 0.02 / 72.0

GRID = 2.46875
WRAP_X = float(np.float32(N_COL * CELL_SIDE) - np.float32(N_COL * GRID))
WRAP_Y = float(np.float32(N_ROW * CELL_SIDE) - np.float32(N_ROW * GRID))

CUT_X = float(np.float32(CUT_SQ + SOFT_CORE))
FEATURES = 32 + 2 * TYPE_PAD
LINK = GROUP + BLOCK
TABLE_V = 64
GROUPS = (
    (0, 0, 256, 0, 256),
    (0, 256, 384, 128, 256),
    (1, 128, 256, 256, 384),
    (1, 256, 512, 256, 512),
)
CHUNK = 128
NT = (((1,), (1,)), ((), ()))


def iota(shape, dim):
    return lax.broadcasted_iota(I32, shape, dim)


def split3(x):
    high = x.astype(BF16).astype(F32)
    rest = x - high
    mid = rest.astype(BF16).astype(F32)
    return high, mid, rest - mid


def kernel(
    pos_hbm, typ_hbm, slot_hbm, pair_hbm, count_hbm, c6_hbm, c12_hbm, out_ref,
    pos_ref, typ_ref, slot_ref, pair_ref, count_ref, c6_ref, c12_ref,
    rec, perm, unperm, stage, pairs, tab, rhs_w, rhs_6, rhs_12, own_z, expand, feat, high, low, acc,
    load_sem, send_sem, recv_sem,
):
    loads = [
        pltpu.make_async_copy(source, target, load_sem.at[n])
        for n, (source, target) in enumerate((
            (slot_hbm, slot_ref), (pos_hbm, pos_ref), (typ_hbm, typ_ref), (pair_hbm, pair_ref),
            (count_hbm, count_ref), (c6_hbm, c6_ref), (c12_hbm, c12_ref),
        ))
    ]
    for load in loads[:5]:
        load.start()

    row, col = lax.axis_index("row"), lax.axis_index("col")
    u = 2 * (col % 8) + col // 8
    v = 2 * (row % 16) + row // 16

    def device_at(e, f):
        to_u = (u + e + N_COL) % N_COL
        to_v = (v + f + N_ROW) % N_ROW
        return (to_v // 2 + to_v % 2 * 16, to_u // 2 + to_u % 2 * 8)

    def slot_of(e, f):
        return (f + 1) * 3 + e + 1

    early = v % 16 == 0
    late = v % 16 == 15
    below = v % 16 == 14
    lower = v % 16 == 13
    last = v == N_ROW - 1
    before_last = v == N_ROW - 2
    even = u % 2 == 0
    half_heard = late & even & jnp.logical_not(last | (u & 13 == 8))
    barrier = pltpu.get_barrier_semaphore()

    def greet(e, f):
        pl.semaphore_signal(barrier, inc=1, device_id=device_at(e, f), device_id_type=MESH)

    greet(0, -1)

    @pl.when(jnp.logical_not(late))
    def _():
        greet(-1, -1)
        greet(1, -1)

    @pl.when(jnp.logical_not(late | before_last))
    def _():
        greet(0, 1)

    for e in (-1, 1):
        to_half_heard = below & jnp.logical_not(even | ((u + e) & 13 == 8))

        @pl.when(jnp.logical_not(late | before_last | lower | to_half_heard))
        def _():
            greet(e, 1)

    @pl.when(jnp.logical_not(late))
    def _():
        greet(-1, 0)
        greet(1, 0)

    for load in loads[5:]:
        load.start()
    loads[0].wait()
    perm[...] = (iota((GROUP, GROUP), 0) == slot_ref[...]).astype(F32).astype(BF16)
    for load in loads[1:5]:
        load.wait()
    stage[...] = jnp.zeros_like(stage)
    stage[0:3, :] = pos_ref[...]
    stage[3:4, :] = typ_ref[...].astype(F32)
    which = iota((8, GROUP), 0)
    lane = iota((8, GROUP), 1)
    layer = lane // BLOCK
    half = GRID * 0.5
    origin = jnp.where(which == 0, u.astype(F32) * GRID + half, 0.0)
    origin = jnp.where(which == 1, v.astype(F32) * GRID + half, origin)
    parts = jnp.concatenate(split3(stage[...] - origin), axis=0).astype(BF16)
    moved = jnp.dot(parts, perm[...], preferred_element_type=F32)
    own = moved[0:8] + moved[8:16] + moved[16:24]
    own = own - jnp.where(which == 2, layer.astype(F32) * GRID + half, 0.0)
    rec[4, :, 0:GROUP] = own[0:4]

    pairs[...] = jnp.zeros_like(pairs)
    pairs[0:2, 0:72] = pair_ref[...]
    code = pairs[...]
    first, second = code[0:1], code[1:2]
    at_a = 2 * ((first >> 2) & 7) + (first >> 5)
    at_b = 2 * ((second >> 2) & 15) + (second >> 6)
    du = (at_a - u + 1) & (N_COL - 1)
    dv = (at_b - v + 1) & (N_ROW - 1)
    ka, kb = first & 3, second & 3
    live = iota((1, BLOCK), 1) < count_ref[0]
    eight = iota((8, BLOCK), 0)
    full = iota((BLOCK, BLOCK), 0)

    left = jnp.concatenate([eight == ka, eight == kb], axis=1)
    left = jnp.where(left & jnp.concatenate([live, live], axis=1), 1.0, 0.0).astype(BF16)
    at_u = du * 16 + dv * 4 + kb
    at_v = TABLE_V + dv * 16 + du * 4 + ka
    right = jnp.concatenate([full == at_u, full == at_v], axis=1)
    right = jnp.where(right, 1.0, 0.0).astype(BF16)
    rec[4, :, GROUP:LINK] = lax.dot_general(left, right, NT, preferred_element_type=F32)[0:4]

    def link(e, f, width=None):
        width = width or (GROUP if e and f else LINK)
        return pltpu.make_async_remote_copy(
            src_ref=rec.at[4, :, pl.ds(0, width)],
            dst_ref=rec.at[slot_of(-e, -f), :, pl.ds(0, width)],
            send_sem=send_sem.at[slot_of(e, f)],
            recv_sem=recv_sem.at[slot_of(-e, -f)],
            device_id=device_at(e, f),
            device_id_type=MESH,
        )

    def forward(e, f, width):
        return pltpu.make_async_remote_copy(
            src_ref=rec.at[slot_of(e, f), :, pl.ds(0, width)],
            dst_ref=rec.at[slot_of(e, f + 1), :, pl.ds(0, width)],
            send_sem=send_sem.at[slot_of(e, -1) if f == 0 else 9 + (e + 1) // 2],
            recv_sem=recv_sem.at[slot_of(e, f + 1)],
            device_id=device_at(0, -1),
            device_id_type=MESH,
        )

    count = lambda flag: flag.astype(I32)
    expected = 8 - 3 * count(early) - 2 * count(late) - 3 * count(last) - 4 * count(below) - 2 * count(half_heard)
    pl.semaphore_wait(barrier, expected)

    @pl.when(late)
    def _():
        link(1, 1, LINK).start()
        link(-1, 1, LINK).start()

    link(0, 1).start()

    @pl.when(jnp.logical_not(late | below))
    def _():
        link(-1, 1).start()
        link(1, 1).start()

    @pl.when(jnp.logical_not(early | last))
    def _():
        link(0, -1).start()

    @pl.when(jnp.logical_not(early | last | half_heard | below))
    def _():
        link(-1, -1).start()
        link(1, -1).start()

    @pl.when(jnp.logical_not(late))
    def _():
        link(-1, 0).start()
        link(1, 0).start()

    row4 = which & 3
    upper = which < 4
    own8 = jnp.concatenate([own[0:4], own[0:4]], axis=0)
    one = jnp.where(row4 == 3, 1.0, 0.0)
    zeros = jnp.zeros((2 * TYPE_PAD, GROUP), F32)
    for p in range(2):
        x = own8 + jnp.where(row4 == 2, (layer.astype(F32) - (2 * p + 0.5)) * GRID, 0.0)
        x = jnp.where(row4 == 3, 0.0, x)
        own_z[p] = x
        norm = jnp.sum(x[0:4] * x[0:4], axis=0, keepdims=True) + SOFT_CORE
        h, m, l = split3(x)
        nh, nm, nl = split3(norm)
        sides = [
            -2.0 * h + one,
            -2.0 * jnp.where(upper, m, h) + jnp.where(upper, 0.0, one),
            -2.0 * jnp.where(upper, l, m),
            jnp.where(which == 0, nh, jnp.where(which == 1, nm, jnp.where(which == 2, nl, 0.0))),
            zeros,
        ]
        rhs_w[p] = jnp.concatenate(sides, axis=0).astype(BF16)

    for load in loads[5:]:
        load.wait()
    kinds = (iota((TYPE_PAD, GROUP), 0).astype(F32) == own[3:4]).astype(F32)
    blank = jnp.zeros((32, GROUP), F32)
    for source, target, factor in ((c6_ref, rhs_6, 6.0), (c12_ref, rhs_12, 12.0)):
        tab[...] = jnp.zeros_like(tab)
        tab[0:NTYPE, 0:NTYPE] = source[...] * factor
        coef = jnp.dot(tab[:, 0:TYPE_PAD], kinds, precision=HIGH, preferred_element_type=F32)
        first_part = coef.astype(BF16).astype(F32)
        target[...] = jnp.concatenate([blank, first_part, coef - first_part], axis=0).astype(BF16)
    wanted = jnp.broadcast_to(slot_ref[...].astype(F32), (8, GROUP)).T[:, 0:1]
    unperm[...] = (iota((GROUP, GROUP), 1).astype(F32) == wanted).astype(F32).astype(BF16)
    expand[...] = (iota((16, GROUP), 0) == iota((16, GROUP), 1) // BLOCK).astype(F32).astype(BF16)
    acc[...] = jnp.zeros_like(acc)

    inv_cut = 1.0 / (CUT_X)
    cut4 = inv_cut**4
    cut7 = inv_cut**7

    ahead = (1 - 2 * (v % 2)) * (1 - 2 * count(before_last))

    def wait(slot, width):
        pltpu.make_async_remote_copy(
            src_ref=rec.at[4, :, pl.ds(0, width)],
            dst_ref=rec.at[slot, :, pl.ds(0, width)],
            send_sem=send_sem.at[slot], recv_sem=recv_sem.at[slot],
            device_id=device_at(1, 0), device_id_type=MESH,
        ).wait_recv()

    def features(slot, at, scale):
        e, f = slot % 3 - 1, slot // 3 - 1
        tab_u = rec[3 + e + 1, :, GROUP:LINK]
        tab_v = rec[(f + 1) * 3 + 1, :, GROUP:LINK]
        shift_u = BLOCK - ((1 - e) * 16 + (1 + f) * 4)
        shift_v = BLOCK - (TABLE_V + (1 - f) * 16 + (1 + e) * 4)
        tab_u = pltpu.roll(jnp.concatenate([tab_u, tab_u], axis=0), shift_u, 1)
        tab_v = pltpu.roll(jnp.concatenate([tab_v, tab_v], axis=0), shift_v, 1)
        seen = (tab_u + tab_v)[:, 0:16]
        weight = jnp.dot(seen.astype(BF16), expand[...], preferred_element_type=F32)
        twice = jnp.where((slot == 4) & (which == layer), 0.5, 1.0)
        weight = weight * twice * scale

        beads = rec[slot, :, 0:GROUP]
        beads = jnp.concatenate([beads, beads], axis=0)
        over_u = (u + e + N_COL) // N_COL - 1
        over_v = (v + f + N_ROW) // N_ROW - 1
        shift_x = e.astype(F32) * GRID + over_u.astype(F32) * WRAP_X
        shift_y = f.astype(F32) * GRID + over_v.astype(F32) * WRAP_Y
        shift_z = ((layer & 1).astype(F32) - 0.5) * GRID
        shift = jnp.where(row4 == 0, shift_x, jnp.where(row4 == 1, shift_y, shift_z))
        x = jnp.where(row4 == 3, 0.0, beads + shift)
        norm = jnp.sum(x[0:4] * x[0:4], axis=0, keepdims=True)
        h, m, l = split3(jnp.where(row4 == 3, norm, x))
        high_mid = jnp.where(upper, h, m)
        kind_row = iota((TYPE_PAD, GROUP), 0).astype(F32)
        onehot = (kind_row == beads[3:4]).astype(F32)
        rows = jnp.concatenate(
            [high_mid, jnp.where(upper, h, l), high_mid, jnp.ones((8, GROUP), F32), onehot, onehot],
            axis=0,
        ).astype(BF16)
        for k in range(BPD):
            feat[at, k * BLOCK : (k + 1) * BLOCK, :] = rows[:, k * BLOCK : (k + 1) * BLOCK].T
        back = jnp.concatenate([high_mid, jnp.where(upper, l, 1.0)], axis=0)
        return back, weight

    def scalars(at):
        for p, m0, m1, n0, n1 in GROUPS:
            for n in range(n0, n1, CHUNK):
                side = feat[at, n : n + CHUNK, :]
                dist = jnp.dot(side, rhs_w[p, :, m0:m1], preferred_element_type=F32)
                c6 = jnp.dot(side, rhs_6[:, m0:m1], preferred_element_type=F32)
                c12 = jnp.dot(side, rhs_12[:, m0:m1], preferred_element_type=F32)
                inv = 1.0 / jnp.minimum(dist, CUT_X)
                inv2 = inv * inv
                inv3 = inv2 * inv
                inv4 = inv2 * inv2
                scalar = c12 * (inv4 * inv3 - cut7) - c6 * (inv4 - cut4)
                rounded = scalar.astype(BF16)
                high[at, n : n + CHUNK, m0:m1] = rounded
                low[at, n : n + CHUNK, m0:m1] = (scalar - rounded.astype(F32)).astype(BF16)

    def sums(at, back, weight):
        for p, m0, m1, n0, n1 in GROUPS:
            layers = range(m0 // BLOCK, m1 // BLOCK)
            pull = jnp.concatenate(
                [back[:, n0:n1] * weight[k : k + 1, n0:n1] for k in layers], axis=0
            ).astype(BF16)
            got = jnp.dot(pull, high[at, n0:n1, m0:m1], preferred_element_type=F32) + jnp.dot(
                pull, low[at, n0:n1, m0:m1], preferred_element_type=F32
            )
            for n, k in enumerate(layers):
                lanes = slice(k * BLOCK, (k + 1) * BLOCK)
                acc[p, :, lanes] += got[16 * n : 16 * n + 16, n * BLOCK : (n + 1) * BLOCK]

    def two_columns(t, carry):
        is_u = (t == 1).astype(I32)
        side_at = 3 - count((v == 0) & (u == 2))
        is_far = (t == 5 - side_at).astype(I32)
        is_side = (t == side_at).astype(I32)
        is_near = (t == 4).astype(I32)
        e = is_u + is_far + is_near
        f = is_far * ahead - is_near * ahead
        one_slot = (f + is_side * ahead + 1) * 3 + 1 - e
        two_slot = (f - is_side * ahead + 1) * 3 + 1 + e

        @pl.when((is_u == 1) & (last | half_heard))
        def _():
            wait(1, LINK)
            link(-1, -1).start()
            link(1, -1).start()

            @pl.when(last)
            def _():
                link(0, -1).start()

        @pl.when(is_u == 1)
        def _():
            wait(one_slot, LINK)
            wait(two_slot, LINK)

            @pl.when(below)
            def _():
                for f in (-1, 1):
                    link(-1, f).start()
                    link(1, f).start()

        @pl.when((t == 2) & jnp.logical_not(last | half_heard))
        def _():
            wait((ahead + 1) * 3 + 1, LINK)

        @pl.when(is_side == 1)
        def _():
            wait((1 - ahead) * 3 + 1, LINK)

            @pl.when(early)
            def _():
                link(0, -1).start()
                forward(-1, 0, GROUP).start()
                forward(1, 0, GROUP).start()

        from_late = (is_near == 1) & early

        @pl.when((is_far + is_near == 1) & jnp.logical_not(from_late))
        def _():
            wait(one_slot, GROUP)
            wait(two_slot, GROUP)

        @pl.when(from_late)
        def _():
            for side in (-1, 1):
                wait(slot_of(side, -1), LINK)
                forward(side, -1, LINK).start()

        scale = jnp.minimum(t, 1).astype(F32)
        first_side = features(one_slot, 0, 1.0)
        second_side = features(two_slot, 1, scale)
        scalars(0)
        sums(0, *first_side)
        scalars(1)
        sums(1, *second_side)
        return carry

    lax.fori_loop(0, 5, two_columns, 0)

    force = jnp.zeros((8, GROUP), F32)
    for p in range(2):
        got = acc[p]
        pulled = got[0:8] + pltpu.roll(got[0:8], 4, 0) + got[8:16]
        force += own_z[p] * got[12:13] - pulled
    force = force * KICK_FACTOR
    coarse = force.astype(BF16).astype(F32)
    parts = jnp.concatenate([coarse, force - coarse], axis=0).astype(BF16)
    stored = jnp.dot(parts, unperm[...], preferred_element_type=F32)
    out_ref[...] = (stored[0:8] + stored[8:16])[0:3]

    for e in (-1, 0, 1):
        link(e, -1).wait_send()
    link(0, 1).wait_send()

    @pl.when(late)
    def _():
        link(-1, 1, LINK).wait_send()
        link(1, 1, LINK).wait_send()

    @pl.when(jnp.logical_not(late))
    def _():
        for e in (-1, 1):
            link(e, 1).wait_send()
            link(e, 0).wait_send()

    @pl.when(early)
    def _():
        forward(-1, -1, LINK).wait_send()
        forward(1, -1, LINK).wait_send()


def body(positions, velocities, bead_types, slot_bead, tile_pairs, tile_count, c6_table, c12_table):
    vmem = pl.BlockSpec(memory_space=pltpu.VMEM)
    hbm = pl.BlockSpec(memory_space=pltpu.HBM)
    kick = pl.pallas_call(
        kernel,
        out_shape=pltpu.VMEM((3, GROUP), F32),
        in_specs=[hbm] * 7,
        out_specs=vmem,
        scratch_shapes=[
            pltpu.VMEM((3, GROUP), F32),
            pltpu.VMEM((1, GROUP), I32),
            pltpu.VMEM((1, GROUP), I32),
            pltpu.VMEM((2, 72), I32),
            pltpu.SMEM((1,), I32),
            pltpu.VMEM((NTYPE, NTYPE), F32),
            pltpu.VMEM((NTYPE, NTYPE), F32),
            pltpu.VMEM((9, 4, LINK), F32),
            pltpu.VMEM((GROUP, GROUP), BF16),
            pltpu.VMEM((GROUP, GROUP), BF16),
            pltpu.VMEM((8, GROUP), F32),
            pltpu.VMEM((8, BLOCK), I32),
            pltpu.VMEM((TYPE_PAD, BLOCK), F32),
            pltpu.VMEM((2, FEATURES, GROUP), BF16),
            pltpu.VMEM((FEATURES, GROUP), BF16),
            pltpu.VMEM((FEATURES, GROUP), BF16),
            pltpu.VMEM((2, 8, GROUP), F32),
            pltpu.VMEM((16, GROUP), BF16),
            pltpu.VMEM((2, GROUP, FEATURES), BF16),
            pltpu.VMEM((2, GROUP, GROUP), BF16),
            pltpu.VMEM((2, GROUP, GROUP), BF16),
            pltpu.VMEM((2, 16, GROUP), F32),
            pltpu.SemaphoreType.DMA((7,)),
            pltpu.SemaphoreType.DMA((11,)),
            pltpu.SemaphoreType.DMA((9,)),
        ],
        compiler_params=pltpu.CompilerParams(
            collective_id=0, has_side_effects=True, vmem_limit_bytes=60 * 2**20
        ),
        name="column_forces",
    )(
        positions,
        bead_types.reshape(1, GROUP),
        slot_bead.reshape(1, GROUP),
        tile_pairs,
        tile_count,
        c6_table,
        c12_table,
    )
    return velocities + kick


def solution(mesh):
    return jax.shard_map(
        body,
        mesh=mesh,
        in_specs=(
            P(None, ("row", "col")),
            P(None, ("row", "col")),
            P(("row", "col")),
            P(("row", "col")),
            P(None, ("row", "col")),
            P(("row", "col")),
            P(),
            P(),
        ),
        out_specs=P(None, ("row", "col")),
        check_vma=False,
    )
```

```python
import functools

import jax
import jax.numpy as jnp
import numpy as np
from jax import lax
from jax.experimental import pallas as pl
from jax.experimental.pallas import tpu as pltpu
from jax.sharding import PartitionSpec as P

F32 = jnp.float32
BF16 = jnp.bfloat16
I32 = jnp.int32
MESH = pl.DeviceIdType.MESH
HIGH = lax.Precision.HIGHEST

BLOCK = 128
BPD = 4
GROUP = BPD * BLOCK
N_ROW = 32
N_COL = 16
NTYPE = 18
TYPE_PAD = 24
SOFT_CORE = 0.25
CUT_SQ = 1.2 * 1.2
CELL_SIDE = 2.47
KICK_FACTOR = 0.02 / 72.0

GRID = 2.46875
WRAP_X = float(np.float32(N_COL * CELL_SIDE) - np.float32(N_COL * GRID))
WRAP_Y = float(np.float32(N_ROW * CELL_SIDE) - np.float32(N_ROW * GRID))

CUT_X = float(np.float32(CUT_SQ + SOFT_CORE))
FEATURES = 32 + 2 * TYPE_PAD
LINK = GROUP + BLOCK
TABLE_V = 64
GROUPS = (
    (0, 0, 256, 0, 256),
    (0, 256, 384, 128, 256),
    (1, 128, 256, 256, 384),
    (1, 256, 512, 256, 512),
)
CHUNK = 128
NT = (((1,), (1,)), ((), ()))


def iota(shape, dim):
    return lax.broadcasted_iota(I32, shape, dim)


def split3(x):
    high = x.astype(BF16).astype(F32)
    rest = x - high
    mid = rest.astype(BF16).astype(F32)
    return high, mid, rest - mid


def kernel(
    pos_hbm, typ_hbm, slot_hbm, pair_hbm, count_hbm, c6_hbm, c12_hbm, out_ref,
    pos_ref, typ_ref, slot_ref, pair_ref, count_ref, c6_ref, c12_ref,
    rec, perm, unperm, stage, pairs, tab, rhs_w, rhs_6, rhs_12, own_z, expand, feat, high, low, acc,
    load_sem, send_sem, recv_sem,
):
    loads = [
        pltpu.make_async_copy(source, target, load_sem.at[n])
        for n, (source, target) in enumerate((
            (slot_hbm, slot_ref), (pos_hbm, pos_ref), (typ_hbm, typ_ref), (pair_hbm, pair_ref),
            (count_hbm, count_ref), (c6_hbm, c6_ref), (c12_hbm, c12_ref),
        ))
    ]
    for load in loads[:5]:
        load.start()

    row, col = lax.axis_index("row"), lax.axis_index("col")
    u = 2 * (col % 8) + col // 8
    v = 2 * (row % 16) + row // 16

    def device_at(e, f):
        to_u = (u + e + N_COL) % N_COL
        to_v = (v + f + N_ROW) % N_ROW
        return (to_v // 2 + to_v % 2 * 16, to_u // 2 + to_u % 2 * 8)

    def slot_of(e, f):
        return (f + 1) * 3 + e + 1

    early = v % 16 == 0
    late = v % 16 == 15
    below = v % 16 == 14
    lower = v % 16 == 13
    last = v == N_ROW - 1
    before_last = v == N_ROW - 2
    even = u % 2 == 0
    half_heard = late & even & jnp.logical_not(last | (u & 13 == 8))
    barrier = pltpu.get_barrier_semaphore()

    def greet(e, f):
        pl.semaphore_signal(barrier, inc=1, device_id=device_at(e, f), device_id_type=MESH)

    greet(0, -1)

    @pl.when(jnp.logical_not(late))
    def _():
        greet(-1, -1)
        greet(1, -1)

    @pl.when(jnp.logical_not(late | before_last))
    def _():
        greet(0, 1)

    for e in (-1, 1):
        to_half_heard = below & jnp.logical_not(even | ((u + e) & 13 == 8))

        @pl.when(jnp.logical_not(late | before_last | lower | to_half_heard))
        def _():
            greet(e, 1)

    @pl.when(jnp.logical_not(late))
    def _():
        greet(-1, 0)
        greet(1, 0)

    for load in loads[5:]:
        load.start()
    loads[0].wait()
    perm[...] = (iota((GROUP, GROUP), 0) == slot_ref[...]).astype(F32).astype(BF16)
    for load in loads[1:5]:
        load.wait()
    stage[...] = jnp.zeros_like(stage)
    stage[0:3, :] = pos_ref[...]
    stage[3:4, :] = typ_ref[...].astype(F32)
    which = iota((8, GROUP), 0)
    lane = iota((8, GROUP), 1)
    layer = lane // BLOCK
    half = GRID * 0.5
    origin = jnp.where(which == 0, u.astype(F32) * GRID + half, 0.0)
    origin = jnp.where(which == 1, v.astype(F32) * GRID + half, origin)
    parts = jnp.concatenate(split3(stage[...] - origin), axis=0).astype(BF16)
    moved = jnp.dot(parts, perm[...], preferred_element_type=F32)
    own = moved[0:8] + moved[8:16] + moved[16:24]
    own = own - jnp.where(which == 2, layer.astype(F32) * GRID + half, 0.0)
    rec[4, :, 0:GROUP] = own[0:4]

    pairs[...] = jnp.zeros_like(pairs)
    pairs[0:2, 0:72] = pair_ref[...]
    code = pairs[...]
    first, second = code[0:1], code[1:2]
    at_a = 2 * ((first >> 2) & 7) + (first >> 5)
    at_b = 2 * ((second >> 2) & 15) + (second >> 6)
    du = (at_a - u + 1) & (N_COL - 1)
    dv = (at_b - v + 1) & (N_ROW - 1)
    ka, kb = first & 3, second & 3
    live = iota((1, BLOCK), 1) < count_ref[0]
    eight = iota((8, BLOCK), 0)
    full = iota((BLOCK, BLOCK), 0)

    left = jnp.concatenate([eight == ka, eight == kb], axis=1)
    left = jnp.where(left & jnp.concatenate([live, live], axis=1), 1.0, 0.0).astype(BF16)
    at_u = du * 16 + dv * 4 + kb
    at_v = TABLE_V + dv * 16 + du * 4 + ka
    right = jnp.concatenate([full == at_u, full == at_v], axis=1)
    right = jnp.where(right, 1.0, 0.0).astype(BF16)
    rec[4, :, GROUP:LINK] = lax.dot_general(left, right, NT, preferred_element_type=F32)[0:4]

    def link(e, f, width=None):
        width = width or (GROUP if e and f else LINK)
        return pltpu.make_async_remote_copy(
            src_ref=rec.at[4, :, pl.ds(0, width)],
            dst_ref=rec.at[slot_of(-e, -f), :, pl.ds(0, width)],
            send_sem=send_sem.at[slot_of(e, f)],
            recv_sem=recv_sem.at[slot_of(-e, -f)],
            device_id=device_at(e, f),
            device_id_type=MESH,
        )

    def forward(e, f, width):
        return pltpu.make_async_remote_copy(
            src_ref=rec.at[slot_of(e, f), :, pl.ds(0, width)],
            dst_ref=rec.at[slot_of(e, f + 1), :, pl.ds(0, width)],
            send_sem=send_sem.at[slot_of(e, -1) if f == 0 else 9 + (e + 1) // 2],
            recv_sem=recv_sem.at[slot_of(e, f + 1)],
            device_id=device_at(0, -1),
            device_id_type=MESH,
        )

    count = lambda flag: flag.astype(I32)
    expected = 8 - 3 * count(early) - 2 * count(late) - 3 * count(last) - 4 * count(below) - 2 * count(half_heard)
    pl.semaphore_wait(barrier, expected)

    @pl.when(late)
    def _():
        link(1, 1, LINK).start()
        link(-1, 1, LINK).start()

    link(0, 1).start()

    @pl.when(jnp.logical_not(late | below))
    def _():
        link(-1, 1).start()
        link(1, 1).start()

    @pl.when(jnp.logical_not(early | last))
    def _():
        link(0, -1).start()

    @pl.when(jnp.logical_not(early | last | half_heard | below))
    def _():
        link(-1, -1).start()
        link(1, -1).start()

    @pl.when(jnp.logical_not(late))
    def _():
        link(-1, 0).start()
        link(1, 0).start()

    row4 = which & 3
    upper = which < 4
    own8 = jnp.concatenate([own[0:4], own[0:4]], axis=0)
    one = jnp.where(row4 == 3, 1.0, 0.0)
    zeros = jnp.zeros((2 * TYPE_PAD, GROUP), F32)
    for p in range(2):
        x = own8 + jnp.where(row4 == 2, (layer.astype(F32) - (2 * p + 0.5)) * GRID, 0.0)
        x = jnp.where(row4 == 3, 0.0, x)
        own_z[p] = x
        norm = jnp.sum(x[0:4] * x[0:4], axis=0, keepdims=True) + SOFT_CORE
        h, m, l = split3(x)
        nh, nm, nl = split3(norm)
        sides = [
            -2.0 * h + one,
            -2.0 * jnp.where(upper, m, h) + jnp.where(upper, 0.0, one),
            -2.0 * jnp.where(upper, l, m),
            jnp.where(which == 0, nh, jnp.where(which == 1, nm, jnp.where(which == 2, nl, 0.0))),
            zeros,
        ]
        rhs_w[p] = jnp.concatenate(sides, axis=0).astype(BF16)

    for load in loads[5:]:
        load.wait()
    kinds = (iota((TYPE_PAD, GROUP), 0).astype(F32) == own[3:4]).astype(F32)
    blank = jnp.zeros((32, GROUP), F32)
    for source, target, factor in ((c6_ref, rhs_6, 6.0), (c12_ref, rhs_12, 12.0)):
        tab[...] = jnp.zeros_like(tab)
        tab[0:NTYPE, 0:NTYPE] = source[...] * factor
        coef = jnp.dot(tab[:, 0:TYPE_PAD], kinds, precision=HIGH, preferred_element_type=F32)
        first_part = coef.astype(BF16).astype(F32)
        target[...] = jnp.concatenate([blank, first_part, coef - first_part], axis=0).astype(BF16)
    wanted = jnp.broadcast_to(slot_ref[...].astype(F32), (8, GROUP)).T[:, 0:1]
    unperm[...] = (iota((GROUP, GROUP), 1).astype(F32) == wanted).astype(F32).astype(BF16)
    expand[...] = (iota((16, GROUP), 0) == iota((16, GROUP), 1) // BLOCK).astype(F32).astype(BF16)
    acc[...] = jnp.zeros_like(acc)

    inv_cut = 1.0 / (CUT_X)
    cut4 = inv_cut**4
    cut7 = inv_cut**7

    ahead = (1 - 2 * (v % 2)) * (1 - 2 * count(before_last))

    def wait(slot, width):
        pltpu.make_async_remote_copy(
            src_ref=rec.at[4, :, pl.ds(0, width)],
            dst_ref=rec.at[slot, :, pl.ds(0, width)],
            send_sem=send_sem.at[slot], recv_sem=recv_sem.at[slot],
            device_id=device_at(1, 0), device_id_type=MESH,
        ).wait_recv()

    def features(slot, at, scale):
        e, f = slot % 3 - 1, slot // 3 - 1
        tab_u = rec[3 + e + 1, :, GROUP:LINK]
        tab_v = rec[(f + 1) * 3 + 1, :, GROUP:LINK]
        shift_u = BLOCK - ((1 - e) * 16 + (1 + f) * 4)
        shift_v = BLOCK - (TABLE_V + (1 - f) * 16 + (1 + e) * 4)
        tab_u = pltpu.roll(jnp.concatenate([tab_u, tab_u], axis=0), shift_u, 1)
        tab_v = pltpu.roll(jnp.concatenate([tab_v, tab_v], axis=0), shift_v, 1)
        seen = (tab_u + tab_v)[:, 0:16]
        weight = jnp.dot(seen.astype(BF16), expand[...], preferred_element_type=F32)
        twice = jnp.where((slot == 4) & (which == layer), 0.5, 1.0)
        weight = weight * twice * scale

        beads = rec[slot, :, 0:GROUP]
        beads = jnp.concatenate([beads, beads], axis=0)
        over_u = (u + e + N_COL) // N_COL - 1
        over_v = (v + f + N_ROW) // N_ROW - 1
        shift_x = e.astype(F32) * GRID + over_u.astype(F32) * WRAP_X
        shift_y = f.astype(F32) * GRID + over_v.astype(F32) * WRAP_Y
        shift_z = ((layer & 1).astype(F32) - 0.5) * GRID
        shift = jnp.where(row4 == 0, shift_x, jnp.where(row4 == 1, shift_y, shift_z))
        x = jnp.where(row4 == 3, 0.0, beads + shift)
        norm = jnp.sum(x[0:4] * x[0:4], axis=0, keepdims=True)
        h, m, l = split3(jnp.where(row4 == 3, norm, x))
        high_mid = jnp.where(upper, h, m)
        kind_row = iota((TYPE_PAD, GROUP), 0).astype(F32)
        onehot = (kind_row == beads[3:4]).astype(F32)
        rows = jnp.concatenate(
            [high_mid, jnp.where(upper, h, l), high_mid, jnp.ones((8, GROUP), F32), onehot, onehot],
            axis=0,
        ).astype(BF16)
        for k in range(BPD):
            feat[at, k * BLOCK : (k + 1) * BLOCK, :] = rows[:, k * BLOCK : (k + 1) * BLOCK].T
        back = jnp.concatenate([high_mid, jnp.where(upper, l, 1.0)], axis=0)
        return back, weight

    def scalars(at):
        for p, m0, m1, n0, n1 in GROUPS:
            for n in range(n0, n1, CHUNK):
                side = feat[at, n : n + CHUNK, :]
                dist = jnp.dot(side, rhs_w[p, :, m0:m1], preferred_element_type=F32)
                c6 = jnp.dot(side, rhs_6[:, m0:m1], preferred_element_type=F32)
                c12 = jnp.dot(side, rhs_12[:, m0:m1], preferred_element_type=F32)
                inv = 1.0 / jnp.minimum(dist, CUT_X)
                inv2 = inv * inv
                inv3 = inv2 * inv
                inv4 = inv2 * inv2
                scalar = c12 * (inv4 * inv3 - cut7) - c6 * (inv4 - cut4)
                rounded = scalar.astype(BF16)
                high[at, n : n + CHUNK, m0:m1] = rounded
                low[at, n : n + CHUNK, m0:m1] = (scalar - rounded.astype(F32)).astype(BF16)

    def sums(at, back, weight):
        for p, m0, m1, n0, n1 in GROUPS:
            layers = range(m0 // BLOCK, m1 // BLOCK)
            pull = jnp.concatenate(
                [back[:, n0:n1] * weight[k : k + 1, n0:n1] for k in layers], axis=0
            ).astype(BF16)
            got = jnp.dot(pull, high[at, n0:n1, m0:m1], preferred_element_type=F32) + jnp.dot(
                pull, low[at, n0:n1, m0:m1], preferred_element_type=F32
            )
            for n, k in enumerate(layers):
                lanes = slice(k * BLOCK, (k + 1) * BLOCK)
                acc[p, :, lanes] += got[16 * n : 16 * n + 16, n * BLOCK : (n + 1) * BLOCK]

    def two_columns(t, carry):
        is_u = (t == 1).astype(I32)
        side_at = 3 - count((v == 0) & (u == 2))
        is_far = (t == 5 - side_at).astype(I32)
        is_side = (t == side_at).astype(I32)
        is_near = (t == 4).astype(I32)
        e = is_u + is_far + is_near
        f = is_far * ahead - is_near * ahead
        one_slot = (f + is_side * ahead + 1) * 3 + 1 - e
        two_slot = (f - is_side * ahead + 1) * 3 + 1 + e

        @pl.when((is_u == 1) & (last | half_heard))
        def _():
            wait(1, LINK)
            link(-1, -1).start()
            link(1, -1).start()

            @pl.when(last)
            def _():
                link(0, -1).start()

        @pl.when(is_u == 1)
        def _():
            wait(one_slot, LINK)
            wait(two_slot, LINK)

            @pl.when(below)
            def _():
                for f in (-1, 1):
                    link(-1, f).start()
                    link(1, f).start()

        @pl.when((t == 2) & jnp.logical_not(last | half_heard))
        def _():
            wait((ahead + 1) * 3 + 1, LINK)

        @pl.when(is_side == 1)
        def _():
            wait((1 - ahead) * 3 + 1, LINK)

            @pl.when(early)
            def _():
                link(0, -1).start()
                forward(-1, 0, GROUP).start()
                forward(1, 0, GROUP).start()

        from_late = (is_near == 1) & early

        @pl.when((is_far + is_near == 1) & jnp.logical_not(from_late))
        def _():
            wait(one_slot, GROUP)
            wait(two_slot, GROUP)

        @pl.when(from_late)
        def _():
            for side in (1, -1):
                wait(slot_of(side, -1), LINK)
                forward(side, -1, LINK).start()

        scale = jnp.minimum(t, 1).astype(F32)
        first_side = features(one_slot, 0, 1.0)
        second_side = features(two_slot, 1, scale)
        scalars(0)
        sums(0, *first_side)
        scalars(1)
        sums(1, *second_side)
        return carry

    lax.fori_loop(0, 5, two_columns, 0)

    force = jnp.zeros((8, GROUP), F32)
    for p in range(2):
        got = acc[p]
        pulled = got[0:8] + pltpu.roll(got[0:8], 4, 0) + got[8:16]
        force += own_z[p] * got[12:13] - pulled
    force = force * KICK_FACTOR
    coarse = force.astype(BF16).astype(F32)
    parts = jnp.concatenate([coarse, force - coarse], axis=0).astype(BF16)
    stored = jnp.dot(parts, unperm[...], preferred_element_type=F32)
    out_ref[...] = (stored[0:8] + stored[8:16])[0:3]

    for e in (-1, 0, 1):
        link(e, -1).wait_send()
    link(0, 1).wait_send()

    @pl.when(late)
    def _():
        link(-1, 1, LINK).wait_send()
        link(1, 1, LINK).wait_send()

    @pl.when(jnp.logical_not(late))
    def _():
        for e in (-1, 1):
            link(e, 1).wait_send()
            link(e, 0).wait_send()

    @pl.when(early)
    def _():
        forward(-1, -1, LINK).wait_send()
        forward(1, -1, LINK).wait_send()


def body(positions, velocities, bead_types, slot_bead, tile_pairs, tile_count, c6_table, c12_table):
    vmem = pl.BlockSpec(memory_space=pltpu.VMEM)
    hbm = pl.BlockSpec(memory_space=pltpu.HBM)
    kick = pl.pallas_call(
        kernel,
        out_shape=pltpu.VMEM((3, GROUP), F32),
        in_specs=[hbm] * 7,
        out_specs=vmem,
        scratch_shapes=[
            pltpu.VMEM((3, GROUP), F32),
            pltpu.VMEM((1, GROUP), I32),
            pltpu.VMEM((1, GROUP), I32),
            pltpu.VMEM((2, 72), I32),
            pltpu.SMEM((1,), I32),
            pltpu.VMEM((NTYPE, NTYPE), F32),
            pltpu.VMEM((NTYPE, NTYPE), F32),
            pltpu.VMEM((9, 4, LINK), F32),
            pltpu.VMEM((GROUP, GROUP), BF16),
            pltpu.VMEM((GROUP, GROUP), BF16),
            pltpu.VMEM((8, GROUP), F32),
            pltpu.VMEM((8, BLOCK), I32),
            pltpu.VMEM((TYPE_PAD, BLOCK), F32),
            pltpu.VMEM((2, FEATURES, GROUP), BF16),
            pltpu.VMEM((FEATURES, GROUP), BF16),
            pltpu.VMEM((FEATURES, GROUP), BF16),
            pltpu.VMEM((2, 8, GROUP), F32),
            pltpu.VMEM((16, GROUP), BF16),
            pltpu.VMEM((2, GROUP, FEATURES), BF16),
            pltpu.VMEM((2, GROUP, GROUP), BF16),
            pltpu.VMEM((2, GROUP, GROUP), BF16),
            pltpu.VMEM((2, 16, GROUP), F32),
            pltpu.SemaphoreType.DMA((7,)),
            pltpu.SemaphoreType.DMA((11,)),
            pltpu.SemaphoreType.DMA((9,)),
        ],
        compiler_params=pltpu.CompilerParams(
            collective_id=0, has_side_effects=True, vmem_limit_bytes=60 * 2**20
        ),
        name="column_forces",
    )(
        positions,
        bead_types.reshape(1, GROUP),
        slot_bead.reshape(1, GROUP),
        tile_pairs,
        tile_count,
        c6_table,
        c12_table,
    )
    return velocities + kick


def solution(mesh):
    return jax.shard_map(
        body,
        mesh=mesh,
        in_specs=(
            P(None, ("row", "col")),
            P(None, ("row", "col")),
            P(("row", "col")),
            P(("row", "col")),
            P(None, ("row", "col")),
            P(("row", "col")),
            P(),
            P(),
        ),
        out_specs=P(None, ("row", "col")),
        check_vma=False,
    )
```
